512 devices in a mesh: band: 64 (over x, z), ens: 8 (over y, core).
Axes of the slice: x: 4, y: 4, z: 16, core: 2. Of those that a mesh axis runs over, the one named last changes fastest.
Arguments:
- state: bfloat16 [8, 114, 368640], P('ens', None, 'band'), may hold values from -6 to 6
- cotangent: bfloat16 [8, 114, 368640], P('ens', None, 'band'), may hold values from -6 to 6
- w_in: bfloat16 [114, 384], replicated, may hold values from -0.5 to 0.5
- b_in: float32 [384], replicated, may hold values from -3 to 3
- w_out: bfloat16 [114, 384], replicated, may hold values from -0.3125 to 0.3125
- legendre: bfloat16 [256, 256, 256], P('band'), may hold values from -2 to 2
- diffusion: float32 [114], replicated, may hold values from 0.3 to 30
- quad: float32 [256], replicated, may hold values from 0.3 to 3
- table: int32 [64, 4], replicated, may hold values from 0 to 255, as said below
Outputs:
- state_grad: bfloat16 [8, 114, 368640], P('ens', None, 'band')
- w_in_grad: float32 [114, 384], replicated
- w_out_grad: float32 [114, 384], replicated
- b_in_grad: float32 [384], replicated
The draws below stay inside these ranges and needn't reach their ends.
Inputs may be any that keep to these rules, and one draw needn't show every extreme that they name: `table`: each wavenumber 0 to 255 appears exactly once. Columns 2g and 2g+1 of every row hold m and (4 g + 2) * 64 - 1 - m for some m with 2 g * 64 <= m < (2 g + 1) * 64, so the sum of 256 - m over the wavenumbers m of a row is the same for every row.
All inputs are finite; a program needn't handle non-finite values.
Results may differ from the reference program's by a relative error of at most 0.018.
Values may be sent and summed in bfloat16 or wider, within the bound.
A program may use at most 64 MiB of HBM per device.

```python
import math
import jax
import jax.numpy as jnp
from jax import lax

NLON = 1440
C = 114
HID = 384
M_DEV = 4
ENS = 8
NLAT = 256
MODES = 256
NDEG = 256
N_BAND = 64


def draw_table(key, part):
    key = jax.random.fold_in(key, 7)
    columns = []
    for group_index in range(M_DEV // 2):
        shuffled = jax.random.permutation(jax.random.fold_in(key, group_index), N_BAND).astype(jnp.int32)
        offset = 2 * N_BAND * group_index
        columns.append(offset + shuffled)
        columns.append(offset + 2 * N_BAND - 1 - shuffled)
    return jnp.stack(columns, axis=1).astype(jnp.int32)


def block_levels(own_key, shape, split, least, high):
    def one(position, blocks):
        steps = jax.random.uniform(jax.random.fold_in(jax.random.fold_in(own_key, 6), position), (blocks,), jnp.float32, least / len(split), high / len(split))
        return jnp.repeat(jnp.exp(steps), shape[position] // blocks).reshape((-1,) + (1,) * (len(shape) - position - 1))

    loudness = one(*split[0])
    for cut in split[1:]:
        loudness = loudness * one(*cut)
    return loudness


def noise(stream_key, extent, spread, reach, split=(), kind=jnp.bfloat16):
    entries = jax.random.normal(stream_key, extent, jnp.float32) * spread
    if len(split) > 0:
        entries = block_levels(stream_key, extent, split, -0.22, 0.18) * entries
    return jnp.clip(entries, min=-reach, max=reach).astype(kind)


def setup_inputs(seed: int = 0) -> dict:
    splits = jax.random.split(jax.random.key(seed), 10)
    return {
        "state": noise(splits[0], (ENS, C, NLAT * NLON), 1.0, 6.0, ((0, 8), (2, 64))),
        "cotangent": noise(splits[1], (ENS, C, NLAT * NLON), 1.0, 6.0, ((0, 8), (2, 64))),
        "w_in": noise(splits[2], (C, HID), C ** -0.5, 0.5),
        "b_in": noise(splits[3], (HID,), 0.5, 3.0, (), jnp.float32),
        "w_out": noise(splits[4], (C, HID), HID ** -0.5, 0.3125),
        "legendre": noise(splits[5], (MODES, NLAT, NDEG), (1.36 * MODES ** -0.5 * (NLON * NLAT ** -1) ** 0.25), 2.0, ((0, 64),)),
        "diffusion": jnp.clip(jnp.exp(jax.random.uniform(splits[6], (C,), jnp.float32, math.log(0.3), math.log(30.0))), 0.3, 30.0),
        "quad": jnp.clip(jnp.exp(jax.random.uniform(splits[7], (NLAT,), jnp.float32, math.log(0.3), math.log(3.0))), 0.3, 3.0),
        "table": draw_table(jax.random.fold_in(splits[9], 71), 0),
    }


def wave_matrix(table):
    wavenumbers = table.reshape(-1).astype(jnp.int32)
    longitude = jnp.arange(NLON, dtype=jnp.int32)
    phase = wavenumbers[:, None] * longitude[None, :] % NLON
    angle = phase.astype(jnp.float32) * (2.0 * math.pi / NLON)
    stacked = jnp.stack([jnp.cos(angle), jnp.sin(angle)], axis=1)
    stacked = stacked.reshape(2 * wavenumbers.shape[0], NLON)
    return (stacked * (1.0 / math.sqrt(NLON))).astype(jnp.bfloat16)

def damping_table(wavenumbers, diffusion, degrees):
    degree = jnp.arange(degrees, dtype=jnp.float32)
    scaled = degree * (degree + 1.0) / (degrees * (degrees - 1.0))
    keeping = (jnp.arange(degrees, dtype=jnp.int32)[None, :] >= wavenumbers[:, None]).astype(jnp.float32)
    return keeping[:, None, :] / (1.0 + diffusion[None, :, None] * (scaled * scaled)[None, None, :])

def reference(state, cotangent, w_in, b_in, w_out, legendre, diffusion, quad, table):
    members = state.shape[0]
    channels = state.shape[1]
    wave_rows = wave_matrix(table).astype(jnp.float32)
    damping = damping_table(table.reshape(-1).astype(jnp.int32), diffusion, NDEG)
    legendre_f = legendre.astype(jnp.float32)

    def analysis(field):
        return jnp.einsum('cln,kn->kcl', field.astype(jnp.float32), wave_rows)

    def synthesis(coefs):
        return jnp.einsum('kcl,kn->cln', coefs.astype(jnp.float32), wave_rows)

    def legendre_pass(piece, weight_after):
        folded = piece.astype(jnp.float32).reshape(MODES, 2 * channels, NLAT)
        summed = jnp.einsum('kcl,kld->kcd', folded, legendre_f)
        spectrum = (summed.reshape(MODES, 2, channels, NDEG) * damping[:, None]).reshape(MODES, 2 * channels, NDEG)
        spectrum = spectrum.astype(jnp.bfloat16)
        result = jnp.einsum('kcd,kld->kcl', spectrum.astype(jnp.float32), legendre_f)
        if weight_after:
            result = result * quad[None, None, :]
        return result.astype(jnp.bfloat16).reshape(2 * MODES, channels, NLAT)

    def forward(member_state):
        field = member_state.reshape(channels, NLAT, NLON)
        coefs = (analysis(field) * quad[None, None, :]).astype(jnp.bfloat16)
        return synthesis(legendre_pass(coefs, False)).astype(jnp.bfloat16)
    grid_state = lax.map(forward, state)
    group = 16
    blocks = NLAT // group
    y_rows = grid_state.reshape(members, channels, blocks, group * NLON).transpose(0, 2, 1, 3)
    y_rows = y_rows.reshape(members * blocks, channels, group * NLON)
    g_rows = cotangent.reshape(members, channels, blocks, group * NLON).transpose(0, 2, 1, 3)
    g_rows = g_rows.reshape(members * blocks, channels, group * NLON)
    w_in_f = w_in.astype(jnp.float32)
    w_out_f = w_out.astype(jnp.float32)

    def column_step(carry, items):
        grad_in, grad_out, grad_bias = carry
        y_cols, g_cols = items
        y_f = y_cols.astype(jnp.float32)
        g_f = g_cols.astype(jnp.float32)
        hidden_pre = jnp.dot(w_in_f.T, y_f, preferred_element_type=jnp.float32) + b_in[:, None]
        sigma = jax.nn.sigmoid(hidden_pre)
        hidden = (hidden_pre * sigma).astype(jnp.bfloat16)
        hidden_grad = jnp.dot(w_out_f.T, g_f, preferred_element_type=jnp.float32)
        pre_grad = (hidden_grad * sigma * (1.0 + hidden_pre * (1.0 - sigma))).astype(jnp.bfloat16)
        pre_f = pre_grad.astype(jnp.float32)
        grad_out = grad_out + jnp.dot(g_f, hidden.astype(jnp.float32).T, preferred_element_type=jnp.float32)
        grad_in = grad_in + jnp.dot(y_f, pre_f.T, preferred_element_type=jnp.float32)
        grad_bias = grad_bias + lax.optimization_barrier(jnp.sum(pre_f, axis=1))
        back_cols = jnp.dot(w_in_f, pre_f, preferred_element_type=jnp.float32).astype(jnp.bfloat16)
        return ((grad_in, grad_out, grad_bias), back_cols)
    start = (jnp.zeros((channels, HID), jnp.float32), jnp.zeros((channels, HID), jnp.float32), jnp.zeros((HID,), jnp.float32))
    sums, back_rows = lax.scan(column_step, start, (y_rows, g_rows))
    back_grid = back_rows.reshape(members, blocks, channels, group * NLON).transpose(0, 2, 1, 3)
    back_grid = back_grid.reshape(members, channels, NLAT * NLON)

    def adjoint(pair):
        member_cot, member_back = pair
        direct_coef = analysis(member_cot.reshape(channels, NLAT, NLON)).astype(jnp.bfloat16)
        physics_coef = analysis(member_back.reshape(channels, NLAT, NLON)).astype(jnp.bfloat16)
        adjoint_coef = (direct_coef.astype(jnp.float32) + physics_coef.astype(jnp.float32)).astype(jnp.bfloat16)
        result = synthesis(legendre_pass(adjoint_coef, True))
        return result.astype(jnp.bfloat16).reshape(channels, NLAT * NLON)
    state_grad = lax.map(adjoint, (cotangent, back_grid))
    scale = 1.0 / math.sqrt(members * NLAT * NLON)
    return (state_grad, sums[0] * scale, sums[1] * scale, sums[2] * scale)
```

```python
import functools
import math

import jax
import jax.numpy as jnp
import numpy as np
from jax import lax
from jax.experimental import pallas as pl
from jax.experimental.pallas import tpu as pltpu
from jax.sharding import PartitionSpec as P

MESH = pl.DeviceIdType.MESH
F32, BF16 = jnp.float32, jnp.bfloat16
NLON = 1440
LATS = 4
LANES = 128
STEP = 11 * LANES
WINDOW = 12 * LANES
CHUNK = 5 * LANES
BLOCK = 16


def trig_table(modes):
    phase = np.outer(np.arange(modes), np.arange(NLON)) % NLON
    angle = phase.astype(np.float64) * (2.0 * math.pi / NLON)
    both = np.stack([np.cos(angle), np.sin(angle)]) / math.sqrt(NLON)
    out = np.zeros((LATS, 2, modes, WINDOW), np.float32)
    for a in range(LATS):
        shift = a * (NLON - STEP)
        out[a, :, :, shift : shift + NLON] = both
    return out.astype(jnp.bfloat16)


def nn(a, b):
    return jnp.dot(a, b, preferred_element_type=F32)


def nt(a, b):
    return lax.dot_general(a, b, (((1,), (1,)), ((), ())), preferred_element_type=F32)


def kernel(
    nx, nz, ne, scale,
    state_hbm, cot_hbm, leg_hbm, trig_hbm, w_in, w_out, bias, diffusion, quad, quad_row, table, table_v,
    grad_hbm, w_in_grad, w_out_grad, b_grad,
    state_raw, cot_raw, leg, trig, wave, state_pad, cot_pad, leg_t, w_in_pad, w_in_t, w_out_t, b_cols, damp,
    quad_cols, hidden_grad, direct, stage, stage_out, back_t, y, hidden, pre_grad, back_grid, out_v, small,
    send, recv, gt, rs1, red1, rs2, zsend, zrecv, agx, full,
    in_sem, out_sem, send_sem, recv_sem, g_send, g_recv, z_send, z_recv,
):
    nb = nx * nz
    me = lax.axis_index("band")
    ens = lax.axis_index("ens")
    my_x, my_z = me // nz, lax.rem(me, nz)
    channels = state_raw.shape[0]
    hid = w_in.shape[1]
    nlat = nb * LATS
    whole = channels // 16 * 16
    cols = state_raw.shape[1]

    loads = [
        pltpu.make_async_copy(trig_hbm, trig, in_sem.at[0]),
        pltpu.make_async_copy(state_hbm.at[0], state_raw, in_sem.at[1]),
        pltpu.make_async_copy(cot_hbm.at[0], cot_raw, in_sem.at[2]),
        pltpu.make_async_copy(leg_hbm, leg, in_sem.at[3]),
    ]
    for load in loads:
        load.start()

    def peer_of(i):
        j, dx = i // nx, lax.rem(i, nx)
        up = (j + 1) // 2
        dz = jnp.where(lax.rem(j, 2) == 1, up, nz - up)
        return lax.rem(my_x + dx, nx) * nz + lax.rem(my_z + dz, nz)

    barrier = pltpu.get_barrier_semaphore()

    def greet_band(i, _):
        pl.semaphore_signal(barrier, inc=1, device_id=(peer_of(i), ens), device_id_type=MESH)
        return 0

    def greet_ens(i, _):
        pl.semaphore_signal(barrier, inc=1, device_id=(me, lax.rem(ens + i, ne)), device_id_type=MESH)
        return 0

    lax.fori_loop(1, nb, greet_band, 0)
    lax.fori_loop(1, ne, greet_ens, 0)

    def exchange(n):
        recv[n, pl.ds(me, 1)] = send[n, pl.ds(me, 1)]

        def one(i, _):
            peer = peer_of(nb - i)
            pltpu.make_async_remote_copy(
                src_ref=send.at[n, peer],
                dst_ref=recv.at[n, me],
                send_sem=send_sem.at[n],
                recv_sem=recv_sem.at[n],
                device_id=(peer, ens),
                device_id_type=MESH,
            ).start()
            return 0

        lax.fori_loop(1, nb, one, 0)

    def arrived(n):
        part = recv.at[n, pl.ds(0, nb - 1)]
        pltpu.make_async_copy(part, part, recv_sem.at[n]).wait()

    def left(n):
        part = send.at[n, pl.ds(0, nb - 1)]
        pltpu.make_async_copy(part, part, send_sem.at[n]).wait()

    def pad_rows(dst, src):
        dst[pl.ds(0, whole), :] = src[pl.ds(0, whole), :]
        dst[pl.ds(whole, 16), :] = jnp.zeros((16, dst.shape[1]), dst.dtype)
        dst[pl.ds(whole, channels - whole), :] = src[pl.ds(whole, channels - whole), :]

    def window(a):
        return pl.ds(a * STEP, WINDOW)

    modes = nb * LATS
    lane = lax.broadcasted_iota(jnp.int32, (nb, modes), 1)
    pick = jnp.concatenate(
        [(table_v[:, pl.ds(s, 1)] == lane).astype(F32) for s in range(LATS)], axis=0
    ).astype(BF16)
    loads[0].wait()
    for a in range(LATS):
        for r in range(2):
            rows = nn(pick, trig[a, r]).astype(BF16)
            for s in range(LATS):
                wave[a, pl.ds((2 * s + r) * nb, nb), :] = rows[s * nb : (s + 1) * nb]
    half = 4 * nb

    loads[1].wait()
    pad_rows(state_pad, state_raw)
    for h in range(2):
        for a in range(LATS):
            coef = nt(wave[a, pl.ds(h * half, half), :], state_pad[:, window(a)]) * quad[me * LATS + a]
            for j in range(4):
                stage[pl.ds(a * 4 + j, nb, stride=BLOCK), :] = coef[j * nb : (j + 1) * nb]
        send[h] = stage[pl.ds(0, nb * BLOCK), :].reshape(nb, BLOCK, LANES).astype(BF16)
        if h == 0:
            pl.semaphore_wait(barrier, nb - 1 + ne - 1)
        exchange(h)

    loads[3].wait()
    for s in range(LATS):
        leg_t[s] = leg[s].astype(F32).T.astype(BF16)
    small[...] = jnp.zeros_like(small)
    small[pl.ds(0, 1), pl.ds(0, channels)] = diffusion[...]
    degree = lax.broadcasted_iota(jnp.int32, (nlat, LANES), 0)
    degree_f = degree.astype(F32)
    scaled = degree_f * (degree_f + 1.0) / (nlat * (nlat - 1.0))
    damp[...] = 1.0 / (1.0 + small[pl.ds(0, 1), :] * (scaled * scaled))
    quad_cols[...] = jnp.broadcast_to(quad_row[...], (LANES, nlat)).T
    b_cols[...] = jnp.broadcast_to(bias[...], (LANES, hid)).T
    pad_rows(w_in_pad, w_out)
    w_out_t[...] = w_in_pad[...].astype(F32).T.astype(BF16)
    pad_rows(w_in_pad, w_in)
    w_in_t[...] = w_in_pad[...].astype(F32).T.astype(BF16)
    loads[2].wait()
    pad_rows(cot_pad, cot_raw)
    for a in range(LATS):
        direct[a] = nt(wave[a], cot_pad[:, window(a)])

    def weigh(i, _):
        at = pl.ds(pl.multiple_of(i * CHUNK, LANES), CHUNK)
        hidden_grad[:, at] = nn(w_out_t[...], cot_pad[:, at])
        return 0

    lax.fori_loop(0, cols // CHUNK, weigh, 0)

    def legendre_half(n, h, offset, stride, weight):
        for sub in range(2):
            s = 2 * h + sub
            lines = jnp.concatenate(
                [stage[pl.ds(offset + 2 * sub + r, nlat, stride=stride), :] for r in range(2)], axis=1
            ).astype(BF16)
            keep = jnp.where(degree >= table[me, s], damp[...], 0.0)
            spectrum = (nn(leg_t[s], lines) * jnp.concatenate([keep, keep], axis=1)).astype(BF16)
            back = nn(leg[s], spectrum)
            for r in range(2):
                part = back[:, r * LANES : (r + 1) * LANES]
                if weight:
                    part = part * quad_cols[...]
                stage_out[pl.ds(2 * sub + r, nlat, stride=4), :] = part
        send[n] = stage_out[...].reshape(nb, BLOCK, LANES).astype(BF16)
        exchange(n)

    def gather_half(n, h):
        arrived(n)
        stage[pl.ds(0, nb * BLOCK), :] = recv[n].astype(F32).reshape(nb * BLOCK, LANES)
        for a in range(LATS):
            rows = jnp.concatenate(
                [stage[pl.ds(a * 4 + j, nb, stride=BLOCK), :] for j in range(4)], axis=0
            )
            back_t[a, :, pl.ds(h * half, half)] = rows.T.astype(BF16)

    def synthesis(write):
        tail = None
        for a in range(LATS):
            lines = nn(back_t[a], wave[a])
            head = lines[:, :LANES] if tail is None else lines[:, :LANES] + tail
            write(a * STEP, head)
            write(a * STEP + LANES, lines[:, LANES:STEP])
            tail = lines[:, STEP:]
        write(LATS * STEP, tail)

    for h in range(2):
        arrived(h)
        stage[pl.ds(0, nb * BLOCK), :] = recv[h].astype(F32).reshape(nb * BLOCK, LANES)
        legendre_half(2 + h, h, 0, 4, False)
    for h in range(2):
        gather_half(2 + h, h)

    def write_y(start, lines):
        row = lax.broadcasted_iota(jnp.int32, lines.shape, 0)
        lines = jnp.where(row < channels, lines, jnp.where(row == channels, 1.0, 0.0))
        y[:, pl.ds(start, lines.shape[1])] = lines.astype(BF16)

    synthesis(write_y)

    def network(i, _):
        at = pl.ds(pl.multiple_of(i * CHUNK, LANES), CHUNK)
        pre = nn(w_in_t[...], y[:, at]) + jnp.concatenate([b_cols[...]] * (CHUNK // LANES), axis=1)
        sigma = 0.5 * jnp.tanh(0.5 * pre) + 0.5
        act = pre * sigma
        grad = (hidden_grad[:, at] * (sigma + act * (1.0 - sigma))).astype(BF16)
        hidden[:, at] = act.astype(BF16)
        pre_grad[:, at] = grad
        back_grid[:, at] = nn(w_in_pad[...], grad).astype(BF16)
        return 0

    chunks = cols // CHUNK
    first = -(-(2 * NLON) // CHUNK)
    for p in range(2):
        lax.fori_loop(0 if p == 0 else first, first if p == 0 else chunks, network, 0)
        for sub in range(2):
            a = 2 * p + sub
            coef = direct[a] + nt(wave[a], back_grid[:, window(a)])
            for k in range(8):
                stage[pl.ds(sub * 8 + k, nb, stride=BLOCK), :] = coef[k * nb : (k + 1) * nb]
        send[4 + p] = stage[pl.ds(0, nb * BLOCK), :].reshape(nb, BLOCK, LANES).astype(BF16)
        exchange(4 + p)

    per_e = 2 * hid // ne
    per_x = per_e // nx
    wide = cols // 5
    gt[...] = jnp.zeros_like(gt)

    def gradients(i, _):
        at = pl.ds(pl.multiple_of(i * wide, LANES), wide)
        g_in = nt(pre_grad[:, at], y[:, at])
        g_out = nt(hidden[:, at], cot_pad[:, at])
        gt[...] += jnp.concatenate([g_in, g_out], axis=0).reshape(gt.shape)
        return 0

    lax.fori_loop(0, 5, gradients, 0)

    def to_ens(src, dst, n):
        def one(i, _):
            other = lax.rem(ens + i, ne)
            pltpu.make_async_remote_copy(
                src_ref=src(other), dst_ref=dst, send_sem=g_send.at[n], recv_sem=g_recv.at[n],
                device_id=(me, other), device_id_type=MESH,
            ).start()
            return 0

        lax.fori_loop(1, ne, one, 0)

    def to_x(src, dst, n):
        def one(i, _):
            other = lax.rem(my_x + i, nx)
            pltpu.make_async_remote_copy(
                src_ref=src(other), dst_ref=dst, send_sem=g_send.at[n], recv_sem=g_recv.at[n],
                device_id=(other * nz + my_z, ens), device_id_type=MESH,
            ).start()
            return 0

        lax.fori_loop(1, nx, one, 0)

    def took(ref, count, sem):
        part = ref.at[pl.ds(0, count)]
        pltpu.make_async_copy(part, part, sem).wait()

    rs1[pl.ds(ens, 1)] = gt[pl.ds(ens, 1)]
    to_ens(lambda other: gt.at[other], rs1.at[ens], 0)
    took(rs1, ne - 1, g_recv.at[0])
    red1[...] = jnp.sum(rs1[...], axis=0).reshape(nx, per_x, LANES)
    rs2[pl.ds(my_x, 1)] = red1[pl.ds(my_x, 1)]
    to_x(lambda other: red1.at[other], rs2.at[my_x], 1)

    for p in range(2):
        arrived(4 + p)
    lines = jnp.concatenate([recv[4].astype(F32), recv[5].astype(F32)], axis=1)
    stage[...] = lines.reshape(2 * nb * BLOCK, LANES)
    for h in range(2):
        legendre_half(6 + h, h, 4 * h, 8, True)

    took(rs2, nx - 1, g_recv.at[1])
    total = jnp.sum(rs2[...], axis=0)
    step, distance = 0, 1
    while distance < nz:
        partner = my_z + distance * (1 - 2 * lax.rem(my_z // distance, 2))
        zsend[step] = total
        copy = pltpu.make_async_remote_copy(
            src_ref=zsend.at[step], dst_ref=zrecv.at[step], send_sem=z_send.at[step],
            recv_sem=z_recv.at[step], device_id=(my_x * nz + partner, ens), device_id_type=MESH,
        )
        copy.start()
        copy.wait()
        total = total + zrecv[step]
        step, distance = step + 1, 2 * distance
    agx[pl.ds(my_x, 1)] = total[None]
    to_x(lambda other: agx.at[my_x], agx.at[my_x], 2)
    took(agx, nx - 1, g_recv.at[2])
    full[pl.ds(ens, 1)] = agx[...].reshape(1, per_e, LANES)
    to_ens(lambda other: full.at[ens], full.at[ens], 3)
    gather_half(6, 0)
    took(full, ne - 1, g_recv.at[3])
    sums = (full[...] * scale).reshape(2 * hid, LANES)
    g_in, g_out = sums[:hid].T, sums[hid:].T
    w_in_grad[...] = g_in[:channels]
    w_out_grad[...] = g_out[:channels]
    b_grad[...] = g_in[channels : channels + 1]

    gather_half(7, 1)

    def write_out(start, lines):
        out_v[:, pl.ds(start, lines.shape[1])] = lines[:channels].astype(BF16)

    synthesis(write_out)
    store = pltpu.make_async_copy(out_v, grad_hbm.at[0], out_sem)
    store.start()
    for n in range(8):
        left(n)
    took(gt, ne - 1, g_send.at[0])
    took(red1, nx - 1, g_send.at[1])
    took(agx, nx - 1, g_send.at[2])
    took(full, ne - 1, g_send.at[3])
    store.wait()


def body(nx, nz, ne, state, cotangent, w_in, b_in, w_out, legendre, diffusion, quad, table):
    nb = nx * nz
    channels, cols = state.shape[1:]
    hid = w_in.shape[1]
    nlat = legendre.shape[1]
    modes = nb * LATS
    per_e = 2 * hid // ne
    per_x = per_e // nx
    steps = max(1, nz.bit_length() - 1)
    scale = 1.0 / math.sqrt(ne * nlat * NLON)
    any_spec = pl.BlockSpec(memory_space=pl.ANY)
    vmem = pl.BlockSpec(memory_space=pltpu.VMEM)
    smem = pl.BlockSpec(memory_space=pltpu.SMEM)
    dma = pltpu.SemaphoreType.DMA
    grad, g_in, g_out, g_b = pl.pallas_call(
        functools.partial(kernel, nx, nz, ne, scale),
        out_shape=(
            jax.ShapeDtypeStruct((1, channels, cols), BF16),
            jax.ShapeDtypeStruct((channels, hid), F32),
            jax.ShapeDtypeStruct((channels, hid), F32),
            jax.ShapeDtypeStruct((1, hid), F32),
        ),
        in_specs=[any_spec] * 4 + [vmem] * 4 + [smem, vmem, smem, vmem],
        out_specs=(any_spec, vmem, vmem, vmem),
        scratch_shapes=[
            pltpu.VMEM((channels, cols), BF16),
            pltpu.VMEM((channels, cols), BF16),
            pltpu.VMEM((LATS, nlat, nlat), BF16),
            pltpu.VMEM((LATS, 2, modes, WINDOW), BF16),
            pltpu.VMEM((LATS, 2 * modes, WINDOW), BF16),
            pltpu.VMEM((LANES, cols), BF16),
            pltpu.VMEM((LANES, cols), BF16),
            pltpu.VMEM((LATS, nlat, nlat), BF16),
            pltpu.VMEM((LANES, hid), BF16),
            pltpu.VMEM((hid, LANES), BF16),
            pltpu.VMEM((hid, LANES), BF16),
            pltpu.VMEM((hid, LANES), F32),
            pltpu.VMEM((nlat, LANES), F32),
            pltpu.VMEM((nlat, LANES), F32),
            pltpu.VMEM((hid, cols), F32),
            pltpu.VMEM((LATS, 2 * modes, LANES), F32),
            pltpu.VMEM((2 * nb * BLOCK, LANES), F32),
            pltpu.VMEM((nb * BLOCK, LANES), F32),
            pltpu.VMEM((LATS, LANES, 2 * modes), BF16),
            pltpu.VMEM((LANES, cols), BF16),
            pltpu.VMEM((hid, cols), BF16),
            pltpu.VMEM((hid, cols), BF16),
            pltpu.VMEM((LANES, cols), BF16),
            pltpu.VMEM((channels, cols), BF16),
            pltpu.VMEM((8, LANES), F32),
            pltpu.VMEM((8, nb, BLOCK, LANES), BF16),
            pltpu.VMEM((8, nb, BLOCK, LANES), BF16),
            pltpu.VMEM((ne, per_e, LANES), F32),
            pltpu.VMEM((ne, per_e, LANES), F32),
            pltpu.VMEM((nx, per_x, LANES), F32),
            pltpu.VMEM((nx, per_x, LANES), F32),
            pltpu.VMEM((steps, per_x, LANES), F32),
            pltpu.VMEM((steps, per_x, LANES), F32),
            pltpu.VMEM((nx, per_x, LANES), F32),
            pltpu.VMEM((ne, per_e, LANES), F32),
            dma((4,)),
            dma,
            dma((8,)),
            dma((8,)),
            dma((4,)),
            dma((4,)),
            dma((steps,)),
            dma((steps,)),
        ],
        compiler_params=pltpu.CompilerParams(
            collective_id=0, has_side_effects=True, vmem_limit_bytes=60 * 1024 * 1024
        ),
    )(
        state, cotangent, legendre, jnp.asarray(trig_table(modes)), w_in, w_out, b_in.reshape(1, hid),
        diffusion.reshape(1, channels), quad, quad.reshape(1, nlat), table, table,
    )
    return grad, g_in, g_out, g_b.reshape(hid)


def solution(mesh):
    nb, ne = mesh.shape["band"], mesh.shape["ens"]
    nx = 4 if nb == 64 else 2
    placed = (
        P("ens", None, "band"),
        P("ens", None, "band"),
        P(),
        P(),
        P(),
        P("band", None, None),
        P(),
        P(),
        P(),
    )
    return jax.shard_map(
        functools.partial(body, nx, nb // nx, ne),
        mesh=mesh,
        in_specs=placed,
        out_specs=(P("ens", None, "band"), P(), P(), P()),
        check_vma=False,
    )
```

```python
import functools
import math

import jax
import jax.numpy as jnp
import numpy as np
from jax import lax
from jax.experimental import pallas as pl
from jax.experimental.pallas import tpu as pltpu
from jax.sharding import PartitionSpec as P

MESH = pl.DeviceIdType.MESH
F32, BF16 = jnp.float32, jnp.bfloat16
NLON = 1440
LATS = 4
LANES = 128
STEP = 11 * LANES
WINDOW = 12 * LANES
CHUNK = 6 * LANES
BLOCK = 16


def trig_table(modes):
    phase = np.outer(np.arange(modes), np.arange(NLON)) % NLON
    angle = phase.astype(np.float64) * (2.0 * math.pi / NLON)
    both = np.stack([np.cos(angle), np.sin(angle)]) / math.sqrt(NLON)
    out = np.zeros((LATS, 2, modes, WINDOW), np.float32)
    for a in range(LATS):
        shift = a * (NLON - STEP)
        out[a, :, :, shift : shift + NLON] = both
    return out.astype(jnp.bfloat16)


def nn(a, b):
    return jnp.dot(a, b, preferred_element_type=F32)


def nt(a, b):
    return lax.dot_general(a, b, (((1,), (1,)), ((), ())), preferred_element_type=F32)


def kernel(
    nx, nz, ne, scale,
    state_hbm, cot_hbm, leg_hbm, trig_hbm, w_in, w_out, bias, diffusion, quad, quad_row, table, table_v,
    grad_hbm, w_in_grad, w_out_grad, b_grad,
    state_raw, cot_raw, leg_raw, trig, wave, state_pad, cot_pad, leg, leg_t, leg_f, w_in_pad, w_in_t, w_out_t, b_cols,
    keep, quad_cols, hidden_grad, direct, stage_0, stage_1, partial, back_t, tail, y, hidden, pre_grad, back_grid,
    out_v, small, picks, send, recv, gt, rs1, red1, rs2, zsend, zrecv, agx, full,
    in_sem, out_sem, send_sem, recv_sem, g_send, g_recv, z_send, z_recv,
):
    nb = nx * nz
    me = lax.axis_index("band")
    ens = lax.axis_index("ens")
    my_x, my_z = me // nz, lax.rem(me, nz)
    channels = state_raw.shape[0]
    hid = w_in.shape[1]
    nlat = nb * LATS
    modes = nb * LATS
    pair = 2 * nb
    whole = channels // 16 * 16
    cols = state_raw.shape[1]
    stage = (stage_0, stage_1)

    load_state = pltpu.make_async_copy(state_hbm.at[0], state_raw, in_sem.at[0])
    load_trig = [pltpu.make_async_copy(trig_hbm.at[a], trig.at[a], in_sem.at[1 + a]) for a in range(LATS)]
    load_cot = pltpu.make_async_copy(cot_hbm.at[0], cot_raw, in_sem.at[5])
    load_leg = pltpu.make_async_copy(leg_hbm, leg_raw, in_sem.at[6])
    for load in (load_state, *load_trig, load_cot, load_leg):
        load.start()

    def peer_of(i):
        j, dx = i // nx, lax.rem(i, nx)
        up = (j + 1) // 2
        dz = jnp.where(lax.rem(j, 2) == 1, up, nz - up)
        return lax.rem(my_x + dx, nx) * nz + lax.rem(my_z + dz, nz)

    barrier = pltpu.get_barrier_semaphore()

    def greet_band(i, _):
        pl.semaphore_signal(barrier, inc=1, device_id=(peer_of(i), ens), device_id_type=MESH)
        return 0

    def greet_ens(i, _):
        pl.semaphore_signal(barrier, inc=1, device_id=(me, lax.rem(ens + i, ne)), device_id_type=MESH)
        return 0

    lax.fori_loop(1, nb, greet_band, 0)
    lax.fori_loop(1, ne, greet_ens, 0)

    def exchange(n, p):
        send[n] = stage[p][...].reshape(nb, BLOCK, LANES).astype(BF16)
        recv[n, pl.ds(me, 1)] = send[n, pl.ds(me, 1)]
        if n == 0:
            pl.semaphore_wait(barrier, nb - 1 + ne - 1)

        def one(i, _):
            peer = peer_of(nb - i)
            pltpu.make_async_remote_copy(
                src_ref=send.at[n, peer],
                dst_ref=recv.at[n, me],
                send_sem=send_sem.at[n],
                recv_sem=recv_sem.at[n],
                device_id=(peer, ens),
                device_id_type=MESH,
            ).start()
            return 0

        lax.fori_loop(1, nb, one, 0)

    def arrived(n, p):
        part = recv.at[n, pl.ds(0, nb - 1)]
        pltpu.make_async_copy(part, part, recv_sem.at[n]).wait()
        stage[p][...] = recv[n].astype(F32).reshape(nb * BLOCK, LANES)

    def left(n):
        part = send.at[n, pl.ds(0, nb - 1)]
        pltpu.make_async_copy(part, part, send_sem.at[n]).wait()

    def rows_of(sub, k):
        return pl.ds(sub * 8 + k, nb, stride=BLOCK)

    def pad_rows(dst, src, at):
        dst[pl.ds(0, whole), at] = src[pl.ds(0, whole), at]
        dst[pl.ds(whole, 16), at] = jnp.zeros((16, at.size), dst.dtype)
        dst[pl.ds(whole, channels - whole), at] = src[pl.ds(whole, channels - whole), at]

    def window(a):
        return pl.ds(a * STEP, WINDOW)

    small[...] = jnp.zeros_like(small)
    small[pl.ds(0, LATS), pl.ds(0, nb)] = table_v[...].astype(F32)
    turned = small[...].T
    lane = lax.broadcasted_iota(jnp.int32, (nb, modes), 1).astype(F32)
    picks[...] = jnp.concatenate(
        [(turned[:nb, s : s + 1] == lane).astype(F32) for s in range(LATS)], axis=0
    ).astype(BF16)

    load_state.wait()
    for p in range(2):
        pad_rows(state_pad, state_raw, pl.ds(p * 2 * STEP, cols - 2 * STEP if p else 2 * STEP + LANES))
        pieces = []
        for sub in range(2):
            a = 2 * p + sub
            load_trig[a].wait()
            coef = nt(trig[a].reshape(2 * modes, WINDOW), state_pad[:, window(a)])
            coef = (coef * quad[me * LATS + a]).astype(BF16)
            pieces += [coef[:modes], coef[modes:]]
        picked = nn(picks[...], jnp.concatenate(pieces, axis=1))
        for sub in range(2):
            for k in range(8):
                s, r = k // 2, k % 2
                at = (2 * sub + r) * LANES
                stage[p][rows_of(sub, k), :] = picked[s * nb : (s + 1) * nb, at : at + LANES]
        exchange(p, p)

    for a in range(LATS):
        for r in range(2):
            rows = nn(picks[...], trig[a, r]).astype(BF16)
            for s in range(LATS):
                wave[a, pl.ds((2 * s + r) * nb, nb), :] = rows[s * nb : (s + 1) * nb]
    load_leg.wait()
    for s in range(LATS):
        sides = []
        for side in range(leg_f.shape[0]):
            side_cols = pl.ds(side * leg_f.shape[2], leg_f.shape[2])
            leg_f[side] = leg_raw[s, :, side_cols].astype(F32)
            sides.append(
                jnp.concatenate([leg_f[side, pl.ds(a, nb, stride=LATS), :] for a in range(LATS)], axis=0)
            )
        ordered = jnp.concatenate(sides, axis=1)
        leg[s] = ordered.astype(BF16)
        leg_t[s] = ordered.T.astype(BF16)
    small[pl.ds(0, 1), :] = jnp.zeros((1, LANES), F32)
    small[pl.ds(0, 1), pl.ds(0, channels)] = diffusion[...]
    degree = lax.broadcasted_iota(jnp.int32, (nlat, LANES), 0)
    degree_f = degree.astype(F32)
    scaled = degree_f * (degree_f + 1.0) / (nlat * (nlat - 1.0))
    damp = 1.0 / (1.0 + small[pl.ds(0, 1), :] * (scaled * scaled))
    for s in range(LATS):
        kept = jnp.where(degree >= table[s, me], damp, 0.0)
        keep[s] = jnp.concatenate([kept, kept], axis=1)
    stage_quad = jnp.broadcast_to(quad_row[...], (LANES, nlat)).T
    quad_cols[0] = stage_quad
    for a in range(LATS):
        quad_cols[1, pl.ds(a * nb, nb), :] = quad_cols[0, pl.ds(a, nb, stride=LATS), :]
    b_cols[...] = jnp.broadcast_to(bias[...].reshape(1, hid), (LANES, hid)).T
    pad_rows(w_in_pad, w_out, pl.ds(0, hid))
    w_out_t[...] = w_in_pad[...].astype(F32).T.astype(BF16)
    pad_rows(w_in_pad, w_in, pl.ds(0, hid))
    w_in_t[...] = w_in_pad[...].astype(F32).T.astype(BF16)
    load_cot.wait()
    pad_rows(cot_pad, cot_raw, pl.ds(0, cols))
    for a in range(LATS):
        direct[a] = nt(wave[a], cot_pad[:, window(a)])
    wide = cols // 5

    def weigh(i, _):
        at = pl.ds(pl.multiple_of(i * wide, LANES), wide)
        hidden_grad[:, at] = nn(w_out_t[...], cot_pad[:, at])
        return 0

    lax.fori_loop(0, 5, weigh, 0)

    def legendre(n, weight):
        def lines(p, s):
            parts = [
                jnp.concatenate([stage[p][rows_of(sub, 2 * s + r), :] for sub in range(2)], axis=0)
                for r in range(2)
            ]
            return jnp.concatenate(parts, axis=1).astype(BF16)

        arrived(n, 0)
        for s in range(LATS):
            partial[s] = nn(leg_t[s, :, pl.ds(0, pair)], lines(0, s))
        arrived(n + 1, 1)
        spectrum = []
        for s in range(LATS):
            summed = partial[s] + nn(leg_t[s, :, pl.ds(pair, pair)], lines(1, s))
            spectrum.append((summed * keep[s]).astype(BF16))
        for p in range(2):
            for s in range(LATS):
                back = nn(leg[s, pl.ds(p * pair, pair), :], spectrum[s])
                for r in range(2):
                    part = back[:, r * LANES : (r + 1) * LANES]
                    if weight:
                        part = part * quad_cols[1, pl.ds(p * pair, pair), :]
                    for sub in range(2):
                        stage[p][rows_of(sub, 2 * s + r), :] = part[sub * nb : (sub + 1) * nb]
            exchange(n + 2 + p, p)

    def synthesis(n, p, write):
        arrived(n, p)
        for sub in range(2):
            rows = jnp.concatenate([stage[p][rows_of(sub, k), :] for k in range(8)], axis=0)
            back_t[sub] = rows.T.astype(BF16)
        held = tail[...] if p else None
        for sub in range(2):
            a = 2 * p + sub
            lines = nn(back_t[sub], wave[a])
            write(a * STEP, lines[:, :LANES] if held is None else lines[:, :LANES] + held)
            write(a * STEP + LANES, lines[:, LANES:STEP])
            held = lines[:, STEP:]
        if p == 0:
            tail[...] = held
        write((2 * p + 2) * STEP, held)

    legendre(0, False)

    def write_y(start, lines):
        row = lax.broadcasted_iota(jnp.int32, lines.shape, 0)
        lines = jnp.where(row < channels, lines, jnp.where(row == channels, 1.0, 0.0))
        y[:, pl.ds(start, lines.shape[1])] = lines.astype(BF16)

    def network(i, _):
        at = pl.ds(pl.multiple_of(i * LANES, LANES), CHUNK)
        pre = nn(w_in_t[...], y[:, at]) + jnp.concatenate([b_cols[...]] * (CHUNK // LANES), axis=1)
        sigma = 0.5 * jnp.tanh(0.5 * pre) + 0.5
        act = pre * sigma
        grad = (hidden_grad[:, at] * (sigma + act * (1.0 - sigma))).astype(BF16)
        hidden[:, at] = act.astype(BF16)
        pre_grad[:, at] = grad
        back_grid[:, at] = nn(w_in_pad[...], grad).astype(BF16)
        return 0

    y[:, pl.ds(2 * STEP + LANES, LANES)] = jnp.zeros((LANES, LANES), BF16)
    tiles = cols // LANES
    per_pair, per_chunk = (tiles + 1) // 2, CHUNK // LANES
    trips = -(-per_pair // per_chunk)
    for p in range(2):
        synthesis(2 + p, p, write_y)
        begin = (tiles - trips * per_chunk) if p else 0
        lax.fori_loop(0, trips, lambda i, c, begin=begin: network(begin + i * per_chunk, c), 0)
        for sub in range(2):
            a = 2 * p + sub
            coef = direct[a] + nt(wave[a], back_grid[:, window(a)])
            for k in range(8):
                stage[p][rows_of(sub, k), :] = coef[k * nb : (k + 1) * nb]
        exchange(4 + p, p)

    per_e = 2 * hid // ne
    per_x = per_e // nx
    gt[...] = jnp.zeros_like(gt)

    def gradients(i, _):
        at = pl.ds(pl.multiple_of(i * wide, LANES), wide)
        g_in = nt(pre_grad[:, at], y[:, at])
        g_out = nt(hidden[:, at], cot_pad[:, at])
        gt[...] += jnp.concatenate([g_in, g_out], axis=0).reshape(gt.shape)
        return 0

    lax.fori_loop(0, 5, gradients, 0)

    def to_ens(src, dst, n):
        def one(i, _):
            other = lax.rem(ens + i, ne)
            pltpu.make_async_remote_copy(
                src_ref=src(other), dst_ref=dst, send_sem=g_send.at[n], recv_sem=g_recv.at[n],
                device_id=(me, other), device_id_type=MESH,
            ).start()
            return 0

        lax.fori_loop(1, ne, one, 0)

    def to_x(src, dst, n):
        def one(i, _):
            other = lax.rem(my_x + i, nx)
            pltpu.make_async_remote_copy(
                src_ref=src(other), dst_ref=dst, send_sem=g_send.at[n], recv_sem=g_recv.at[n],
                device_id=(other * nz + my_z, ens), device_id_type=MESH,
            ).start()
            return 0

        lax.fori_loop(1, nx, one, 0)

    def to_z(step):
        distance = 1 << step
        partner = my_z + distance * (1 - 2 * lax.rem(my_z // distance, 2))
        return pltpu.make_async_remote_copy(
            src_ref=zsend.at[step], dst_ref=zrecv.at[step], send_sem=z_send.at[step],
            recv_sem=z_recv.at[step], device_id=(my_x * nz + partner, ens), device_id_type=MESH,
        )

    def took(ref, count, sem):
        part = ref.at[pl.ds(0, count)]
        pltpu.make_async_copy(part, part, sem).wait()

    rs1[pl.ds(ens, 1)] = gt[pl.ds(ens, 1)]
    to_ens(lambda other: gt.at[other], rs1.at[ens], 0)
    took(rs1, ne - 1, g_recv.at[0])
    red1[...] = jnp.sum(rs1[...], axis=0).reshape(nx, per_x, LANES)
    rs2[pl.ds(my_x, 1)] = red1[pl.ds(my_x, 1)]
    to_x(lambda other: red1.at[other], rs2.at[my_x], 1)
    took(rs2, nx - 1, g_recv.at[1])
    zsend[0] = jnp.sum(rs2[...], axis=0)
    to_z(0).start()

    legendre(4, True)

    steps = nz.bit_length() - 1
    for step in range(steps):
        to_z(step).wait()
        total = zsend[step] + zrecv[step]
        if step + 1 < steps:
            zsend[step + 1] = total
            to_z(step + 1).start()
    agx[pl.ds(my_x, 1)] = total[None]
    to_x(lambda other: agx.at[my_x], agx.at[my_x], 2)
    took(agx, nx - 1, g_recv.at[2])
    full[pl.ds(ens, 1)] = agx[...].reshape(1, per_e, LANES)
    to_ens(lambda other: full.at[ens], full.at[ens], 3)

    def write_out(start, lines):
        out_v[:, pl.ds(start, lines.shape[1])] = lines[:channels].astype(BF16)

    synthesis(6, 0, write_out)
    first = pl.ds(0, 2 * STEP)
    store_0 = pltpu.make_async_copy(out_v.at[:, first], grad_hbm.at[0, :, first], out_sem.at[0])
    store_0.start()
    took(full, ne - 1, g_recv.at[3])
    sums = (full[...] * scale).reshape(2 * hid, LANES)
    g_in, g_out = sums[:hid].T, sums[hid:].T
    w_in_grad[...] = g_in[:channels]
    w_out_grad[...] = g_out[:channels]
    b_grad[...] = g_in[channels]
    for n in range(6):
        left(n)
    took(gt, ne - 1, g_send.at[0])
    took(red1, nx - 1, g_send.at[1])
    took(agx, nx - 1, g_send.at[2])
    took(full, ne - 1, g_send.at[3])

    synthesis(7, 1, write_out)
    second = pl.ds(2 * STEP, cols - 2 * STEP)
    store_1 = pltpu.make_async_copy(out_v.at[:, second], grad_hbm.at[0, :, second], out_sem.at[1])
    store_1.start()
    left(6)
    left(7)
    store_0.wait()
    store_1.wait()


def body(nx, nz, ne, state, cotangent, w_in, b_in, w_out, legendre, diffusion, quad, table):
    nb = nx * nz
    channels, cols = state.shape[1:]
    hid = w_in.shape[1]
    nlat = legendre.shape[1]
    modes = nb * LATS
    per_e = 2 * hid // ne
    per_x = per_e // nx
    steps = max(1, nz.bit_length() - 1)
    scale = 1.0 / math.sqrt(ne * nlat * NLON)
    any_spec = pl.BlockSpec(memory_space=pl.ANY)
    vmem = pl.BlockSpec(memory_space=pltpu.VMEM)
    smem = pl.BlockSpec(memory_space=pltpu.SMEM)
    dma = pltpu.SemaphoreType.DMA
    grad, g_in, g_out, g_b = pl.pallas_call(
        functools.partial(kernel, nx, nz, ne, scale),
        out_shape=(
            jax.ShapeDtypeStruct((1, channels, cols), BF16),
            jax.ShapeDtypeStruct((channels, hid), F32),
            jax.ShapeDtypeStruct((channels, hid), F32),
            jax.ShapeDtypeStruct((hid,), F32),
        ),
        in_specs=[any_spec] * 4 + [vmem] * 4 + [smem, vmem, smem, vmem],
        out_specs=(any_spec, vmem, vmem, vmem),
        scratch_shapes=[
            pltpu.VMEM((channels, cols), BF16),
            pltpu.VMEM((channels, cols), BF16),
            pltpu.VMEM((LATS, nlat, nlat), BF16),
            pltpu.VMEM((LATS, 2, modes, WINDOW), BF16),
            pltpu.VMEM((LATS, 2 * modes, WINDOW), BF16),
            pltpu.VMEM((LANES, cols), BF16),
            pltpu.VMEM((LANES, cols), BF16),
            pltpu.VMEM((LATS, nlat, nlat), BF16),
            pltpu.VMEM((LATS, nlat, nlat), BF16),
            pltpu.VMEM((max(1, nlat // LANES), nlat, min(LANES, nlat)), F32),
            pltpu.VMEM((LANES, hid), BF16),
            pltpu.VMEM((hid, LANES), BF16),
            pltpu.VMEM((hid, LANES), BF16),
            pltpu.VMEM((hid, LANES), F32),
            pltpu.VMEM((LATS, nlat, 2 * LANES), F32),
            pltpu.VMEM((2, nlat, LANES), F32),
            pltpu.VMEM((hid, cols), F32),
            pltpu.VMEM((LATS, 2 * modes, LANES), F32),
            pltpu.VMEM((nb * BLOCK, LANES), F32),
            pltpu.VMEM((nb * BLOCK, LANES), F32),
            pltpu.VMEM((LATS, nlat, 2 * LANES), F32),
            pltpu.VMEM((2, LANES, 2 * modes), BF16),
            pltpu.VMEM((LANES, LANES), F32),
            pltpu.VMEM((LANES, cols), BF16),
            pltpu.VMEM((hid, cols), BF16),
            pltpu.VMEM((hid, cols), BF16),
            pltpu.VMEM((LANES, cols), BF16),
            pltpu.VMEM((channels, cols), BF16),
            pltpu.VMEM((8, LANES), F32),
            pltpu.VMEM((LATS * nb, modes), BF16),
            pltpu.VMEM((8, nb, BLOCK, LANES), BF16),
            pltpu.VMEM((8, nb, BLOCK, LANES), BF16),
            pltpu.VMEM((ne, per_e, LANES), F32),
            pltpu.VMEM((ne, per_e, LANES), F32),
            pltpu.VMEM((nx, per_x, LANES), F32),
            pltpu.VMEM((nx, per_x, LANES), F32),
            pltpu.VMEM((steps, per_x, LANES), F32),
            pltpu.VMEM((steps, per_x, LANES), F32),
            pltpu.VMEM((nx, per_x, LANES), F32),
            pltpu.VMEM((ne, per_e, LANES), F32),
            dma((7,)),
            dma((2,)),
            dma((8,)),
            dma((8,)),
            dma((4,)),
            dma((4,)),
            dma((steps,)),
            dma((steps,)),
        ],
        compiler_params=pltpu.CompilerParams(
            collective_id=0, has_side_effects=True, vmem_limit_bytes=60 * 1024 * 1024
        ),
    )(
        state, cotangent, legendre, jnp.asarray(trig_table(modes)), w_in, w_out, b_in,
        diffusion.reshape(1, channels), quad, quad.reshape(1, nlat), table.T, table.T,
    )
    return grad, g_in, g_out, g_b


def solution(mesh):
    nb, ne = mesh.shape["band"], mesh.shape["ens"]
    nx = 4 if nb == 64 else 2
    placed = (
        P("ens", None, "band"),
        P("ens", None, "band"),
        P(),
        P(),
        P(),
        P("band", None, None),
        P(),
        P(),
        P(),
    )
    return jax.shard_map(
        functools.partial(body, nx, nb // nx, ne),
        mesh=mesh,
        in_specs=placed,
        out_specs=(P("ens", None, "band"), P(), P(), P()),
        check_vma=False,
    )
```

```python
import functools
import math

import jax
import jax.numpy as jnp
import numpy as np
from jax import lax
from jax.experimental import pallas as pl
from jax.experimental.pallas import tpu as pltpu
from jax.sharding import PartitionSpec as P

MESH = pl.DeviceIdType.MESH
F32, BF16 = jnp.float32, jnp.bfloat16
NLON = 1440
LATS = 4
LANES = 128
STEP = 11 * LANES
WINDOW = 12 * LANES
CHUNK = 6 * LANES
BLOCK = 16


def trig_table(modes):
    phase = np.outer(np.arange(modes), np.arange(NLON)) % NLON
    angle = phase.astype(np.float64) * (2.0 * math.pi / NLON)
    both = np.stack([np.cos(angle), np.sin(angle)]) / math.sqrt(NLON)
    out = np.zeros((LATS, 2, modes, WINDOW), np.float32)
    for a in range(LATS):
        shift = a * (NLON - STEP)
        out[a, :, :, shift : shift + NLON] = both
    return out.astype(jnp.bfloat16)


def nn(a, b):
    return jnp.dot(a, b, preferred_element_type=F32)


def nt(a, b):
    return lax.dot_general(a, b, (((1,), (1,)), ((), ())), preferred_element_type=F32)


def kernel(
    nx, nz, ne, scale,
    state_hbm, cot_hbm, leg_hbm, trig_hbm, w_in, w_out, bias, diffusion, quad, quad_row, table, table_v,
    grad_hbm, w_in_grad, w_out_grad, b_grad,
    state_raw, cot_raw, leg_raw, trig, wave, state_pad, cot_pad, leg, leg_t, leg_f, w_in_pad, w_in_t, w_out_t, b_cols,
    keep, quad_cols, hidden_grad, direct, stage_0, stage_1, partial, back_t, tail, y, hidden, pre_grad, back_grid,
    out_v, small, picks, send, recv, gt, rs1, red1, rs2, zsend, zrecv, agx, full,
    in_sem, out_sem, send_sem, recv_sem, g_send, g_recv, z_send, z_recv,
):
    nb = nx * nz
    me = lax.axis_index("band")
    ens = lax.axis_index("ens")
    my_x, my_z = me // nz, lax.rem(me, nz)
    channels = state_raw.shape[0]
    hid = w_in.shape[1]
    nlat = nb * LATS
    modes = nb * LATS
    pair = 2 * nb
    whole = channels // 16 * 16
    cols = state_raw.shape[1]
    stage = (stage_0, stage_1)

    load_state = pltpu.make_async_copy(state_hbm.at[0], state_raw, in_sem.at[0])
    load_trig = [pltpu.make_async_copy(trig_hbm.at[a], trig.at[a], in_sem.at[1 + a]) for a in range(LATS)]
    load_cot = pltpu.make_async_copy(cot_hbm.at[0], cot_raw, in_sem.at[5])
    load_leg = pltpu.make_async_copy(leg_hbm, leg_raw, in_sem.at[6])
    for load in (load_state, *load_trig, load_cot, load_leg):
        load.start()

    def peer_of(i):
        j, dx = i // nx, lax.rem(i, nx)
        up = (j + 1) // 2
        dz = jnp.where(lax.rem(j, 2) == 1, up, nz - up)
        return lax.rem(my_x + dx, nx) * nz + lax.rem(my_z + dz, nz)

    barrier = pltpu.get_barrier_semaphore()

    def greet_band(i, _):
        pl.semaphore_signal(barrier, inc=1, device_id=(peer_of(i), ens), device_id_type=MESH)
        return 0

    def greet_ens(i, _):
        pl.semaphore_signal(barrier, inc=1, device_id=(me, lax.rem(ens + i, ne)), device_id_type=MESH)
        return 0

    lax.fori_loop(1, nb, greet_band, 0)
    lax.fori_loop(1, ne, greet_ens, 0)

    def prepare(n, p):
        send[n] = stage[p][...].reshape(nb, BLOCK, LANES).astype(BF16)
        recv[n, pl.ds(me, 1)] = send[n, pl.ds(me, 1)]

    def start(n, first, last):
        def one(i, _):
            peer = peer_of(nb - i)
            pltpu.make_async_remote_copy(
                src_ref=send.at[n, peer],
                dst_ref=recv.at[n, me],
                send_sem=send_sem.at[n],
                recv_sem=recv_sem.at[n],
                device_id=(peer, ens),
                device_id_type=MESH,
            ).start()
            return 0

        lax.fori_loop(first, last, one, 0)

    def arrived(n, p):
        part = recv.at[n, pl.ds(0, nb - 1)]
        pltpu.make_async_copy(part, part, recv_sem.at[n]).wait()
        stage[p][...] = recv[n].astype(F32).reshape(nb * BLOCK, LANES)

    def left(n):
        part = send.at[n, pl.ds(0, nb - 1)]
        pltpu.make_async_copy(part, part, send_sem.at[n]).wait()

    def rows_of(sub, k):
        return pl.ds(sub * 8 + k, nb, stride=BLOCK)

    def pad_rows(dst, src, at):
        dst[pl.ds(0, whole), at] = src[pl.ds(0, whole), at]
        dst[pl.ds(whole, 16), at] = jnp.zeros((16, at.size), dst.dtype)
        dst[pl.ds(whole, channels - whole), at] = src[pl.ds(whole, channels - whole), at]

    def window(a):
        return pl.ds(a * STEP, WINDOW)

    small[...] = jnp.zeros_like(small)
    small[pl.ds(0, LATS), pl.ds(0, nb)] = table_v[...].astype(F32)
    turned = small[...].T
    lane = lax.broadcasted_iota(jnp.int32, (nb, modes), 1).astype(F32)
    picks[...] = jnp.concatenate(
        [(turned[:nb, s : s + 1] == lane).astype(F32) for s in range(LATS)], axis=0
    ).astype(BF16)

    load_state.wait()
    for p in range(2):
        pad_rows(state_pad, state_raw, pl.ds(p * 2 * STEP, cols - 2 * STEP if p else 2 * STEP + LANES))
        pieces = []
        for sub in range(2):
            a = 2 * p + sub
            load_trig[a].wait()
            coef = nt(trig[a].reshape(2 * modes, WINDOW), state_pad[:, window(a)])
            coef = (coef * quad[me * LATS + a]).astype(BF16)
            pieces += [coef[:modes], coef[modes:]]
        picked = nn(picks[...], jnp.concatenate(pieces, axis=1))
        for sub in range(2):
            for k in range(8):
                s, r = k // 2, k % 2
                at = (2 * sub + r) * LANES
                stage[p][rows_of(sub, k), :] = picked[s * nb : (s + 1) * nb, at : at + LANES]
        prepare(p, p)
        if p == 0:
            pl.semaphore_wait(barrier, nb - 1 + ne - 1)
        start(p, 1, nb)

    for a in range(LATS):
        for r in range(2):
            rows = nn(picks[...], trig[a, r]).astype(BF16)
            for s in range(LATS):
                wave[a, pl.ds((2 * s + r) * nb, nb), :] = rows[s * nb : (s + 1) * nb]
    load_leg.wait()
    for s in range(LATS):
        sides = []
        for side in range(leg_f.shape[0]):
            side_cols = pl.ds(side * leg_f.shape[2], leg_f.shape[2])
            leg_f[side] = leg_raw[s, :, side_cols].astype(F32)
            sides.append(
                jnp.concatenate([leg_f[side, pl.ds(a, nb, stride=LATS), :] for a in range(LATS)], axis=0)
            )
        ordered = jnp.concatenate(sides, axis=1)
        leg[s] = ordered.astype(BF16)
        leg_t[s] = ordered.T.astype(BF16)
    small[pl.ds(0, 1), :] = jnp.zeros((1, LANES), F32)
    small[pl.ds(0, 1), pl.ds(0, channels)] = diffusion[...]
    degree = lax.broadcasted_iota(jnp.int32, (nlat, LANES), 0)
    degree_f = degree.astype(F32)
    scaled = degree_f * (degree_f + 1.0) / (nlat * (nlat - 1.0))
    damp = 1.0 / (1.0 + small[pl.ds(0, 1), :] * (scaled * scaled))
    for s in range(LATS):
        kept = jnp.where(degree >= table[s, me], damp, 0.0)
        keep[s] = jnp.concatenate([kept, kept], axis=1)
    stage_quad = jnp.broadcast_to(quad_row[...], (LANES, nlat)).T
    quad_cols[0] = stage_quad
    for a in range(LATS):
        quad_cols[1, pl.ds(a * nb, nb), :] = quad_cols[0, pl.ds(a, nb, stride=LATS), :]
    b_cols[...] = jnp.broadcast_to(bias[...].reshape(1, hid), (LANES, hid)).T
    pad_rows(w_in_pad, w_out, pl.ds(0, hid))
    w_out_t[...] = w_in_pad[...].astype(F32).T.astype(BF16)
    pad_rows(w_in_pad, w_in, pl.ds(0, hid))
    w_in_t[...] = w_in_pad[...].astype(F32).T.astype(BF16)
    load_cot.wait()
    pad_rows(cot_pad, cot_raw, pl.ds(0, cols))
    for a in range(LATS):
        direct[a] = nt(wave[a], cot_pad[:, window(a)])
    wide = cols // 5

    def weigh(i, _):
        at = pl.ds(pl.multiple_of(i * wide, LANES), wide)
        hidden_grad[:, at] = nn(w_out_t[...], cot_pad[:, at])
        return 0

    lax.fori_loop(0, 5, weigh, 0)

    def legendre(n, weight, between=None):
        def lines(p, s):
            parts = [
                jnp.concatenate([stage[p][rows_of(sub, 2 * s + r), :] for sub in range(2)], axis=0)
                for r in range(2)
            ]
            return jnp.concatenate(parts, axis=1).astype(BF16)

        arrived(n, 0)
        for s in range(LATS):
            partial[s] = nn(leg_t[s, :, pl.ds(0, pair)], lines(0, s))
        if between is not None:
            between()
        arrived(n + 1, 1)
        spectrum = []
        for s in range(LATS):
            summed = partial[s] + nn(leg_t[s, :, pl.ds(pair, pair)], lines(1, s))
            spectrum.append((summed * keep[s]).astype(BF16))
        for p in range(2):
            for s in range(LATS):
                back = nn(leg[s, pl.ds(p * pair, pair), :], spectrum[s])
                for r in range(2):
                    part = back[:, r * LANES : (r + 1) * LANES]
                    if weight:
                        part = part * quad_cols[1, pl.ds(p * pair, pair), :]
                    for sub in range(2):
                        stage[p][rows_of(sub, 2 * s + r), :] = part[sub * nb : (sub + 1) * nb]
            prepare(n + 2 + p, p)
            if between is None:
                start(n + 2 + p, 1, nb)

    def synthesis(n, p, write):
        arrived(n, p)
        for sub in range(2):
            rows = jnp.concatenate([stage[p][rows_of(sub, k), :] for k in range(8)], axis=0)
            back_t[sub] = rows.T.astype(BF16)
        held = tail[...] if p else None
        for sub in range(2):
            a = 2 * p + sub
            lines = nn(back_t[sub], wave[a])
            write(a * STEP, lines[:, :LANES] if held is None else lines[:, :LANES] + held)
            write(a * STEP + LANES, lines[:, LANES:STEP])
            held = lines[:, STEP:]
        if p == 0:
            tail[...] = held
        write((2 * p + 2) * STEP, held)

    legendre(0, False)

    def write_y(start, lines):
        row = lax.broadcasted_iota(jnp.int32, lines.shape, 0)
        lines = jnp.where(row < channels, lines, jnp.where(row == channels, 1.0, 0.0))
        y[:, pl.ds(start, lines.shape[1])] = lines.astype(BF16)

    def network(i, _):
        at = pl.ds(pl.multiple_of(i * LANES, LANES), CHUNK)
        pre = nn(w_in_t[...], y[:, at]) + jnp.concatenate([b_cols[...]] * (CHUNK // LANES), axis=1)
        sigma = 0.5 * jnp.tanh(0.5 * pre) + 0.5
        act = pre * sigma
        grad = (hidden_grad[:, at] * (sigma + act * (1.0 - sigma))).astype(BF16)
        hidden[:, at] = act.astype(BF16)
        pre_grad[:, at] = grad
        back_grid[:, at] = nn(w_in_pad[...], grad).astype(BF16)
        return 0

    y[:, pl.ds(2 * STEP + LANES, LANES)] = jnp.zeros((LANES, LANES), BF16)
    tiles = cols // LANES
    per_pair, per_chunk = (tiles + 1) // 2, CHUNK // LANES
    trips = -(-per_pair // per_chunk)
    for p in range(2):
        synthesis(2 + p, p, write_y)
        begin = (tiles - trips * per_chunk) if p else 0
        lax.fori_loop(0, trips, lambda i, c, begin=begin: network(begin + i * per_chunk, c), 0)
        for sub in range(2):
            a = 2 * p + sub
            coef = direct[a] + nt(wave[a], back_grid[:, window(a)])
            for k in range(8):
                stage[p][rows_of(sub, k), :] = coef[k * nb : (k + 1) * nb]
        prepare(4 + p, p)
        start(4 + p, 1, nb if p == 0 else nb // 2)

    per_e = 2 * hid // ne
    per_x = per_e // nx
    gt[...] = jnp.zeros_like(gt)

    def gradients(i, _):
        at = pl.ds(pl.multiple_of(i * wide, LANES), wide)
        g_in = nt(pre_grad[:, at], y[:, at])
        g_out = nt(hidden[:, at], cot_pad[:, at])
        gt[...] += jnp.concatenate([g_in, g_out], axis=0).reshape(gt.shape)
        return 0

    lax.fori_loop(0, 5, gradients, 0)

    def to_ens(src, dst, n):
        def one(i, _):
            other = lax.rem(ens + i, ne)
            pltpu.make_async_remote_copy(
                src_ref=src(other), dst_ref=dst, send_sem=g_send.at[n], recv_sem=g_recv.at[n],
                device_id=(me, other), device_id_type=MESH,
            ).start()
            return 0

        lax.fori_loop(1, ne, one, 0)

    def to_x(src, dst, n):
        def one(i, _):
            other = lax.rem(my_x + i, nx)
            pltpu.make_async_remote_copy(
                src_ref=src(other), dst_ref=dst, send_sem=g_send.at[n], recv_sem=g_recv.at[n],
                device_id=(other * nz + my_z, ens), device_id_type=MESH,
            ).start()
            return 0

        lax.fori_loop(1, nx, one, 0)

    z_sizes = (4, nz // 4)

    def to_z(step, value):
        stride = 4**step
        digit = lax.rem(my_z // stride, z_sizes[step])
        zrecv[step, pl.ds(digit, 1)] = value[None]
        zsend[step] = value

        def one(i, _):
            other = my_z + (lax.rem(digit + i, z_sizes[step]) - digit) * stride
            pltpu.make_async_remote_copy(
                src_ref=zsend.at[step], dst_ref=zrecv.at[step, digit], send_sem=z_send.at[step],
                recv_sem=z_recv.at[step], device_id=(my_x * nz + other, ens), device_id_type=MESH,
            ).start()
            return 0

        lax.fori_loop(1, z_sizes[step], one, 0)

    def from_z(step):
        if z_sizes[step] > 1:
            took(zrecv.at[step], z_sizes[step] - 1, z_recv.at[step])
        return jnp.sum(zrecv[step, pl.ds(0, z_sizes[step])], axis=0)

    def took(ref, count, sem):
        part = ref.at[pl.ds(0, count)]
        pltpu.make_async_copy(part, part, sem).wait()

    rs1[pl.ds(ens, 1)] = gt[pl.ds(ens, 1)]
    to_ens(lambda other: gt.at[other], rs1.at[ens], 0)
    start(5, nb // 2, nb)

    def scatter_x():
        took(rs1, ne - 1, g_recv.at[0])
        red1[...] = jnp.sum(rs1[...], axis=0).reshape(nx, per_x, LANES)
        rs2[pl.ds(my_x, 1)] = red1[pl.ds(my_x, 1)]
        to_x(lambda other: red1.at[other], rs2.at[my_x], 1)

    legendre(4, True, scatter_x)
    start(6, 1, nb // 4)
    took(rs2, nx - 1, g_recv.at[1])
    to_z(0, jnp.sum(rs2[...], axis=0))
    start(6, nb // 4, nb // 2)
    to_z(1, from_z(0))
    start(6, nb // 2, nb)
    agx[pl.ds(my_x, 1)] = from_z(1)[None]
    to_x(lambda other: agx.at[my_x], agx.at[my_x], 2)
    start(7, 1, nb // 2)
    took(agx, nx - 1, g_recv.at[2])
    full[pl.ds(ens, 1)] = agx[...].reshape(1, per_e, LANES)
    to_ens(lambda other: full.at[ens], full.at[ens], 3)
    start(7, nb // 2, nb)

    def write_out(start, lines):
        out_v[:, pl.ds(start, lines.shape[1])] = lines[:channels].astype(BF16)

    synthesis(6, 0, write_out)
    first = pl.ds(0, 2 * STEP)
    store_0 = pltpu.make_async_copy(out_v.at[:, first], grad_hbm.at[0, :, first], out_sem.at[0])
    store_0.start()
    took(full, ne - 1, g_recv.at[3])
    sums = (full[...] * scale).reshape(2 * hid, LANES)
    g_in, g_out = sums[:hid].T, sums[hid:].T
    w_in_grad[...] = g_in[:channels]
    w_out_grad[...] = g_out[:channels]
    b_grad[...] = g_in[channels]
    for n in range(6):
        left(n)
    took(gt, ne - 1, g_send.at[0])
    took(red1, nx - 1, g_send.at[1])
    took(agx, nx - 1, g_send.at[2])
    took(full, ne - 1, g_send.at[3])
    for step in range(2):
        if z_sizes[step] > 1:
            took(zrecv.at[step], z_sizes[step] - 1, z_send.at[step])

    synthesis(7, 1, write_out)
    second = pl.ds(2 * STEP, cols - 2 * STEP)
    store_1 = pltpu.make_async_copy(out_v.at[:, second], grad_hbm.at[0, :, second], out_sem.at[1])
    store_1.start()
    left(6)
    left(7)
    store_0.wait()
    store_1.wait()


def body(nx, nz, ne, state, cotangent, w_in, b_in, w_out, legendre, diffusion, quad, table):
    nb = nx * nz
    channels, cols = state.shape[1:]
    hid = w_in.shape[1]
    nlat = legendre.shape[1]
    modes = nb * LATS
    per_e = 2 * hid // ne
    per_x = per_e // nx
    scale = 1.0 / math.sqrt(ne * nlat * NLON)
    any_spec = pl.BlockSpec(memory_space=pl.ANY)
    vmem = pl.BlockSpec(memory_space=pltpu.VMEM)
    smem = pl.BlockSpec(memory_space=pltpu.SMEM)
    dma = pltpu.SemaphoreType.DMA
    grad, g_in, g_out, g_b = pl.pallas_call(
        functools.partial(kernel, nx, nz, ne, scale),
        out_shape=(
            jax.ShapeDtypeStruct((1, channels, cols), BF16),
            jax.ShapeDtypeStruct((channels, hid), F32),
            jax.ShapeDtypeStruct((channels, hid), F32),
            jax.ShapeDtypeStruct((hid,), F32),
        ),
        in_specs=[any_spec] * 4 + [vmem] * 4 + [smem, vmem, smem, vmem],
        out_specs=(any_spec, vmem, vmem, vmem),
        scratch_shapes=[
            pltpu.VMEM((channels, cols), BF16),
            pltpu.VMEM((channels, cols), BF16),
            pltpu.VMEM((LATS, nlat, nlat), BF16),
            pltpu.VMEM((LATS, 2, modes, WINDOW), BF16),
            pltpu.VMEM((LATS, 2 * modes, WINDOW), BF16),
            pltpu.VMEM((LANES, cols), BF16),
            pltpu.VMEM((LANES, cols), BF16),
            pltpu.VMEM((LATS, nlat, nlat), BF16),
            pltpu.VMEM((LATS, nlat, nlat), BF16),
            pltpu.VMEM((max(1, nlat // LANES), nlat, min(LANES, nlat)), F32),
            pltpu.VMEM((LANES, hid), BF16),
            pltpu.VMEM((hid, LANES), BF16),
            pltpu.VMEM((hid, LANES), BF16),
            pltpu.VMEM((hid, LANES), F32),
            pltpu.VMEM((LATS, nlat, 2 * LANES), F32),
            pltpu.VMEM((2, nlat, LANES), F32),
            pltpu.VMEM((hid, cols), F32),
            pltpu.VMEM((LATS, 2 * modes, LANES), F32),
            pltpu.VMEM((nb * BLOCK, LANES), F32),
            pltpu.VMEM((nb * BLOCK, LANES), F32),
            pltpu.VMEM((LATS, nlat, 2 * LANES), F32),
            pltpu.VMEM((2, LANES, 2 * modes), BF16),
            pltpu.VMEM((LANES, LANES), F32),
            pltpu.VMEM((LANES, cols), BF16),
            pltpu.VMEM((hid, cols), BF16),
            pltpu.VMEM((hid, cols), BF16),
            pltpu.VMEM((LANES, cols), BF16),
            pltpu.VMEM((channels, cols), BF16),
            pltpu.VMEM((8, LANES), F32),
            pltpu.VMEM((LATS * nb, modes), BF16),
            pltpu.VMEM((8, nb, BLOCK, LANES), BF16),
            pltpu.VMEM((8, nb, BLOCK, LANES), BF16),
            pltpu.VMEM((ne, per_e, LANES), F32),
            pltpu.VMEM((ne, per_e, LANES), F32),
            pltpu.VMEM((nx, per_x, LANES), F32),
            pltpu.VMEM((nx, per_x, LANES), F32),
            pltpu.VMEM((2, per_x, LANES), F32),
            pltpu.VMEM((2, 4, per_x, LANES), F32),
            pltpu.VMEM((nx, per_x, LANES), F32),
            pltpu.VMEM((ne, per_e, LANES), F32),
            dma((7,)),
            dma((2,)),
            dma((8,)),
            dma((8,)),
            dma((4,)),
            dma((4,)),
            dma((2,)),
            dma((2,)),
        ],
        compiler_params=pltpu.CompilerParams(
            collective_id=0, has_side_effects=True, vmem_limit_bytes=60 * 1024 * 1024
        ),
    )(
        state, cotangent, legendre, jnp.asarray(trig_table(modes)), w_in, w_out, b_in,
        diffusion.reshape(1, channels), quad, quad.reshape(1, nlat), table.T, table.T,
    )
    return grad, g_in, g_out, g_b


def solution(mesh):
    nb, ne = mesh.shape["band"], mesh.shape["ens"]
    nx = 4 if nb == 64 else 2
    placed = (
        P("ens", None, "band"),
        P("ens", None, "band"),
        P(),
        P(),
        P(),
        P("band", None, None),
        P(),
        P(),
        P(),
    )
    return jax.shard_map(
        functools.partial(body, nx, nb // nx, ne),
        mesh=mesh,
        in_specs=placed,
        out_specs=(P("ens", None, "band"), P(), P(), P()),
        check_vma=False,
    )
```

```python
import functools
import math

import jax
import jax.numpy as jnp
import numpy as np
from jax import lax
from jax.experimental import pallas as pl
from jax.experimental.pallas import tpu as pltpu
from jax.sharding import PartitionSpec as P

MESH = pl.DeviceIdType.MESH
F32, BF16 = jnp.float32, jnp.bfloat16
NLON = 1440
LATS = 4
LANES = 128
STEP = 11 * LANES
WINDOW = 12 * LANES
CHUNK = 6 * LANES
BLOCK = 16


def trig_table(modes):
    phase = np.outer(np.arange(modes), np.arange(NLON)) % NLON
    angle = phase.astype(np.float64) * (2.0 * math.pi / NLON)
    both = np.stack([np.cos(angle), np.sin(angle)]) / math.sqrt(NLON)
    out = np.zeros((LATS, 2, modes, WINDOW), np.float32)
    for a in range(LATS):
        shift = a * (NLON - STEP)
        out[a, :, :, shift : shift + NLON] = both
    return out.astype(jnp.bfloat16)


def nn(a, b):
    return jnp.dot(a, b, preferred_element_type=F32)


def nt(a, b):
    return lax.dot_general(a, b, (((1,), (1,)), ((), ())), preferred_element_type=F32)


def kernel(
    nx, nz, ne, scale,
    state_hbm, cot_hbm, leg_hbm, trig_hbm, w_in, w_out, bias, diffusion, quad, quad_row, table, table_v,
    grad_hbm, w_in_grad, w_out_grad, b_grad,
    state_raw, cot_raw, leg_raw, trig, wave, state_pad, cot_pad, leg, leg_t, leg_f, w_in_pad, w_in_t, w_out_t, b_cols,
    keep, quad_cols, hidden_grad, direct, stage_0, stage_1, partial, back_t, tail, y, hidden, pre_grad, back_grid,
    out_v, small, picks, send, recv, gt, rs1, red1, rs2, zsend, zrecv, agx, full,
    in_sem, out_sem, send_sem, recv_sem, g_send, g_recv, z_send, z_recv,
):
    nb = nx * nz
    me = lax.axis_index("band")
    ens = lax.axis_index("ens")
    my_x, my_z = me // nz, lax.rem(me, nz)
    channels = state_raw.shape[0]
    hid = w_in.shape[1]
    nlat = nb * LATS
    modes = nb * LATS
    pair = 2 * nb
    whole = channels // 16 * 16
    cols = state_raw.shape[1]
    stage = (stage_0, stage_1)

    load_state = pltpu.make_async_copy(state_hbm.at[0], state_raw, in_sem.at[0])
    load_trig = [pltpu.make_async_copy(trig_hbm.at[a], trig.at[a], in_sem.at[1 + a]) for a in range(LATS)]
    load_cot = pltpu.make_async_copy(cot_hbm.at[0], cot_raw, in_sem.at[5])
    load_leg = pltpu.make_async_copy(leg_hbm, leg_raw, in_sem.at[6])
    for load in (load_state, *load_trig[:2]):
        load.start()

    def peer_of(i):
        j, dx = i // nx, lax.rem(i, nx)
        up = (j + 1) // 2
        dz = jnp.where(lax.rem(j, 2) == 1, up, nz - up)
        return lax.rem(my_x + dx, nx) * nz + lax.rem(my_z + dz, nz)

    barrier = pltpu.get_barrier_semaphore()

    def greet_band(i, _):
        pl.semaphore_signal(barrier, inc=1, device_id=(peer_of(i), ens), device_id_type=MESH)
        return 0

    def greet_ens(i, _):
        pl.semaphore_signal(barrier, inc=1, device_id=(me, lax.rem(ens + i, ne)), device_id_type=MESH)
        return 0

    lax.fori_loop(1, nb, greet_band, 0)
    lax.fori_loop(1, ne, greet_ens, 0)

    def prepare(n, p):
        send[n] = stage[p][...].reshape(nb, BLOCK, LANES).astype(BF16)
        recv[n, pl.ds(me, 1)] = send[n, pl.ds(me, 1)]

    def start(n, first, last):
        def one(i, _):
            peer = peer_of(nb - i)
            pltpu.make_async_remote_copy(
                src_ref=send.at[n, peer],
                dst_ref=recv.at[n, me],
                send_sem=send_sem.at[n],
                recv_sem=recv_sem.at[n],
                device_id=(peer, ens),
                device_id_type=MESH,
            ).start()
            return 0

        lax.fori_loop(first, last, one, 0)

    def arrived(n, p):
        part = recv.at[n, pl.ds(0, nb - 1)]
        pltpu.make_async_copy(part, part, recv_sem.at[n]).wait()
        stage[p][...] = recv[n].astype(F32).reshape(nb * BLOCK, LANES)

    def left(n):
        part = send.at[n, pl.ds(0, nb - 1)]
        pltpu.make_async_copy(part, part, send_sem.at[n]).wait()

    def rows_of(sub, k):
        return pl.ds(sub * 8 + k, nb, stride=BLOCK)

    def pad_rows(dst, src, at):
        dst[pl.ds(0, whole), at] = src[pl.ds(0, whole), at]
        dst[pl.ds(whole, 16), at] = jnp.zeros((16, at.size), dst.dtype)
        dst[pl.ds(whole, channels - whole), at] = src[pl.ds(whole, channels - whole), at]

    def window(a):
        return pl.ds(a * STEP, WINDOW)

    small[...] = jnp.zeros_like(small)
    small[pl.ds(0, LATS), pl.ds(0, nb)] = table_v[...].astype(F32)
    turned = small[...].T
    lane = lax.broadcasted_iota(jnp.int32, (nb, modes), 1).astype(F32)
    picks[...] = jnp.concatenate(
        [(turned[:nb, s : s + 1] == lane).astype(F32) for s in range(LATS)], axis=0
    ).astype(BF16)

    load_state.wait()
    for p in range(2):
        pad_rows(state_pad, state_raw, pl.ds(p * 2 * STEP, cols - 2 * STEP if p else 2 * STEP + LANES))
        pieces = []
        for sub in range(2):
            a = 2 * p + sub
            load_trig[a].wait()
            if a == 1:
                for load in (*load_trig[2:], load_leg, load_cot):
                    load.start()
            coef = nt(trig[a].reshape(2 * modes, WINDOW), state_pad[:, window(a)])
            coef = (coef * quad[me * LATS + a]).astype(BF16)
            pieces += [coef[:modes], coef[modes:]]
        picked = nn(picks[...], jnp.concatenate(pieces, axis=1))
        for sub in range(2):
            for k in range(8):
                s, r = k // 2, k % 2
                at = (2 * sub + r) * LANES
                stage[p][rows_of(sub, k), :] = picked[s * nb : (s + 1) * nb, at : at + LANES]
        prepare(p, p)
        if p == 0:
            pl.semaphore_wait(barrier, nb - 1 + ne - 1)
        start(p, 1, nb)

    for a in range(LATS):
        for r in range(2):
            rows = nn(picks[...], trig[a, r]).astype(BF16)
            for s in range(LATS):
                wave[a, pl.ds((2 * s + r) * nb, nb), :] = rows[s * nb : (s + 1) * nb]
    load_leg.wait()
    for s in range(LATS):
        sides = []
        for side in range(leg_f.shape[0]):
            side_cols = pl.ds(side * leg_f.shape[2], leg_f.shape[2])
            leg_f[side] = leg_raw[s, :, side_cols].astype(F32)
            sides.append(
                jnp.concatenate([leg_f[side, pl.ds(a, nb, stride=LATS), :] for a in range(LATS)], axis=0)
            )
        ordered = jnp.concatenate(sides, axis=1)
        leg[s] = ordered.astype(BF16)
        leg_t[s] = ordered.T.astype(BF16)
    small[pl.ds(0, 1), :] = jnp.zeros((1, LANES), F32)
    small[pl.ds(0, 1), pl.ds(0, channels)] = diffusion[...]
    degree = lax.broadcasted_iota(jnp.int32, (nlat, LANES), 0)
    degree_f = degree.astype(F32)
    scaled = degree_f * (degree_f + 1.0) / (nlat * (nlat - 1.0))
    damp = 1.0 / (1.0 + small[pl.ds(0, 1), :] * (scaled * scaled))
    for s in range(LATS):
        kept = jnp.where(degree >= table[s, me], damp, 0.0)
        keep[s] = jnp.concatenate([kept, kept], axis=1)
    stage_quad = jnp.broadcast_to(quad_row[...], (LANES, nlat)).T
    quad_cols[0] = stage_quad
    for a in range(LATS):
        quad_cols[1, pl.ds(a * nb, nb), :] = quad_cols[0, pl.ds(a, nb, stride=LATS), :]
    b_cols[...] = jnp.broadcast_to(bias[...].reshape(1, hid), (LANES, hid)).T
    pad_rows(w_in_pad, w_out, pl.ds(0, hid))
    w_out_t[...] = w_in_pad[...].astype(F32).T.astype(BF16)
    pad_rows(w_in_pad, w_in, pl.ds(0, hid))
    w_in_t[...] = w_in_pad[...].astype(F32).T.astype(BF16)
    load_cot.wait()
    pad_rows(cot_pad, cot_raw, pl.ds(0, cols))
    for a in range(LATS):
        direct[a] = nt(wave[a], cot_pad[:, window(a)])
    wide = cols // 5

    def weigh(i, _):
        at = pl.ds(pl.multiple_of(i * wide, LANES), wide)
        hidden_grad[:, at] = nn(w_out_t[...], cot_pad[:, at])
        return 0

    lax.fori_loop(0, 5, weigh, 0)

    def legendre(n, weight, between=None, first=nb):
        def lines(p, s):
            parts = [
                jnp.concatenate([stage[p][rows_of(sub, 2 * s + r), :] for sub in range(2)], axis=0)
                for r in range(2)
            ]
            return jnp.concatenate(parts, axis=1).astype(BF16)

        arrived(n, 0)
        for s in range(LATS):
            partial[s] = nn(leg_t[s, :, pl.ds(0, pair)], lines(0, s))
        if between is not None:
            between()
        arrived(n + 1, 1)
        spectrum = []
        for s in range(LATS):
            summed = partial[s] + nn(leg_t[s, :, pl.ds(pair, pair)], lines(1, s))
            spectrum.append((summed * keep[s]).astype(BF16))
        for p in range(2):
            for s in range(LATS):
                back = nn(leg[s, pl.ds(p * pair, pair), :], spectrum[s])
                for r in range(2):
                    part = back[:, r * LANES : (r + 1) * LANES]
                    if weight:
                        part = part * quad_cols[1, pl.ds(p * pair, pair), :]
                    for sub in range(2):
                        stage[p][rows_of(sub, 2 * s + r), :] = part[sub * nb : (sub + 1) * nb]
            prepare(n + 2 + p, p)
            if p == 0 or between is None:
                start(n + 2 + p, 1, first)

    def synthesis(n, p, write):
        arrived(n, p)
        for sub in range(2):
            rows = jnp.concatenate([stage[p][rows_of(sub, k), :] for k in range(8)], axis=0)
            back_t[sub] = rows.T.astype(BF16)
        held = tail[...] if p else None
        for sub in range(2):
            a = 2 * p + sub
            lines = nn(back_t[sub], wave[a])
            write(a * STEP, lines[:, :LANES] if held is None else lines[:, :LANES] + held)
            write(a * STEP + LANES, lines[:, LANES:STEP])
            held = lines[:, STEP:]
        if p == 0:
            tail[...] = held
        write((2 * p + 2) * STEP, held)

    legendre(0, False)

    def write_y(start, lines):
        row = lax.broadcasted_iota(jnp.int32, lines.shape, 0)
        lines = jnp.where(row < channels, lines, jnp.where(row == channels, 1.0, 0.0))
        y[:, pl.ds(start, lines.shape[1])] = lines.astype(BF16)

    def network(i, _):
        at = pl.ds(pl.multiple_of(i * LANES, LANES), CHUNK)
        pre = nn(w_in_t[...], y[:, at]) + jnp.concatenate([b_cols[...]] * (CHUNK // LANES), axis=1)
        sigma = 0.5 * jnp.tanh(0.5 * pre) + 0.5
        act = pre * sigma
        grad = (hidden_grad[:, at] * (sigma + act * (1.0 - sigma))).astype(BF16)
        hidden[:, at] = act.astype(BF16)
        pre_grad[:, at] = grad
        back_grid[:, at] = nn(w_in_pad[...], grad).astype(BF16)
        return 0

    per_e = 2 * hid // ne
    per_x = per_e // nx
    gt[...] = jnp.zeros_like(gt)

    def gradients(begin, width):
        def one(i, _):
            at = pl.ds(pl.multiple_of(begin + i * width, LANES), width)
            g_in = nt(pre_grad[:, at], y[:, at])
            g_out = nt(hidden[:, at], cot_pad[:, at])
            gt[...] += jnp.concatenate([g_in, g_out], axis=0).reshape(gt.shape)
            return 0

        lax.fori_loop(0, 3, one, 0)

    y[:, pl.ds(2 * STEP + LANES, LANES)] = jnp.zeros((LANES, LANES), BF16)
    tiles = cols // LANES
    per_pair, per_chunk = (tiles + 1) // 2, CHUNK // LANES
    trips = -(-per_pair // per_chunk)
    for p in range(2):
        synthesis(2 + p, p, write_y)
        begin = (tiles - trips * per_chunk) if p else 0
        lax.fori_loop(0, trips, lambda i, c, begin=begin: network(begin + i * per_chunk, c), 0)
        for sub in range(2):
            a = 2 * p + sub
            coef = direct[a] + nt(wave[a], back_grid[:, window(a)])
            for k in range(8):
                stage[p][rows_of(sub, k), :] = coef[k * nb : (k + 1) * nb]
        prepare(4 + p, p)
        if p == 0:
            start(4, 1, nb)
            gradients(0, (tiles - trips * per_chunk) * LANES // 3)
        else:
            gradients(begin * LANES, trips * CHUNK // 3)

    def to_ens(src, dst, n):
        def one(i, _):
            other = lax.rem(ens + i, ne)
            pltpu.make_async_remote_copy(
                src_ref=src(other), dst_ref=dst, send_sem=g_send.at[n], recv_sem=g_recv.at[n],
                device_id=(me, other), device_id_type=MESH,
            ).start()
            return 0

        lax.fori_loop(1, ne, one, 0)

    def to_x(src, dst, n):
        def one(i, _):
            other = lax.rem(my_x + i, nx)
            pltpu.make_async_remote_copy(
                src_ref=src(other), dst_ref=dst, send_sem=g_send.at[n], recv_sem=g_recv.at[n],
                device_id=(other * nz + my_z, ens), device_id_type=MESH,
            ).start()
            return 0

        lax.fori_loop(1, nx, one, 0)

    z_sizes = (4, nz // 4)

    def to_z(step, value):
        stride = 4**step
        digit = lax.rem(my_z // stride, z_sizes[step])
        zrecv[step, pl.ds(digit, 1)] = value[None]
        zsend[step] = value

        def one(i, _):
            other = my_z + (lax.rem(digit + i, z_sizes[step]) - digit) * stride
            pltpu.make_async_remote_copy(
                src_ref=zsend.at[step], dst_ref=zrecv.at[step, digit], send_sem=z_send.at[step],
                recv_sem=z_recv.at[step], device_id=(my_x * nz + other, ens), device_id_type=MESH,
            ).start()
            return 0

        lax.fori_loop(1, z_sizes[step], one, 0)

    def from_z(step):
        if z_sizes[step] > 1:
            took(zrecv.at[step], z_sizes[step] - 1, z_recv.at[step])
        return jnp.sum(zrecv[step, pl.ds(0, z_sizes[step])], axis=0)

    def took(ref, count, sem):
        part = ref.at[pl.ds(0, count)]
        pltpu.make_async_copy(part, part, sem).wait()

    rs1[pl.ds(ens, 1)] = gt[pl.ds(ens, 1)]
    to_ens(lambda other: gt.at[other], rs1.at[ens], 0)
    start(5, 1, 5 * nb // 8)
    took(rs1, ne - 1, g_recv.at[0])
    red1[...] = jnp.sum(rs1[...], axis=0).reshape(nx, per_x, LANES)
    rs2[pl.ds(my_x, 1)] = red1[pl.ds(my_x, 1)]
    to_x(lambda other: red1.at[other], rs2.at[my_x], 1)
    start(5, 5 * nb // 8, nb)

    def first_z():
        took(rs2, nx - 1, g_recv.at[1])
        to_z(0, jnp.sum(rs2[...], axis=0))

    legendre(4, True, first_z, 3 * nb // 8)
    to_z(1, from_z(0))
    start(6, 3 * nb // 8, 7 * nb // 8)
    agx[pl.ds(my_x, 1)] = from_z(1)[None]
    to_x(lambda other: agx.at[my_x], agx.at[my_x], 2)
    start(6, 7 * nb // 8, nb)
    start(7, 1, nb // 2)
    took(agx, nx - 1, g_recv.at[2])
    full[pl.ds(ens, 1)] = agx[...].reshape(1, per_e, LANES)
    to_ens(lambda other: full.at[ens], full.at[ens], 3)
    start(7, nb // 2, nb)

    def write_out(start, lines):
        out_v[:, pl.ds(start, lines.shape[1])] = lines[:channels].astype(BF16)

    synthesis(6, 0, write_out)
    first = pl.ds(0, 2 * STEP)
    store_0 = pltpu.make_async_copy(out_v.at[:, first], grad_hbm.at[0, :, first], out_sem.at[0])
    store_0.start()
    took(full, ne - 1, g_recv.at[3])
    sums = (full[...] * scale).reshape(2 * hid, LANES)
    g_in, g_out = sums[:hid].T, sums[hid:].T
    w_in_grad[...] = g_in[:channels]
    w_out_grad[...] = g_out[:channels]
    b_grad[...] = g_in[channels]
    for n in range(6):
        left(n)
    took(gt, ne - 1, g_send.at[0])
    took(red1, nx - 1, g_send.at[1])
    took(agx, nx - 1, g_send.at[2])
    took(full, ne - 1, g_send.at[3])
    for step in range(2):
        if z_sizes[step] > 1:
            took(zrecv.at[step], z_sizes[step] - 1, z_send.at[step])

    synthesis(7, 1, write_out)
    second = pl.ds(2 * STEP, cols - 2 * STEP)
    store_1 = pltpu.make_async_copy(out_v.at[:, second], grad_hbm.at[0, :, second], out_sem.at[1])
    store_1.start()
    left(6)
    left(7)
    store_0.wait()
    store_1.wait()


def body(nx, nz, ne, state, cotangent, w_in, b_in, w_out, legendre, diffusion, quad, table):
    nb = nx * nz
    channels, cols = state.shape[1:]
    hid = w_in.shape[1]
    nlat = legendre.shape[1]
    modes = nb * LATS
    per_e = 2 * hid // ne
    per_x = per_e // nx
    scale = 1.0 / math.sqrt(ne * nlat * NLON)
    any_spec = pl.BlockSpec(memory_space=pl.ANY)
    vmem = pl.BlockSpec(memory_space=pltpu.VMEM)
    smem = pl.BlockSpec(memory_space=pltpu.SMEM)
    dma = pltpu.SemaphoreType.DMA
    grad, g_in, g_out, g_b = pl.pallas_call(
        functools.partial(kernel, nx, nz, ne, scale),
        out_shape=(
            jax.ShapeDtypeStruct((1, channels, cols), BF16),
            jax.ShapeDtypeStruct((channels, hid), F32),
            jax.ShapeDtypeStruct((channels, hid), F32),
            jax.ShapeDtypeStruct((hid,), F32),
        ),
        in_specs=[any_spec] * 4 + [vmem] * 4 + [smem, vmem, smem, vmem],
        out_specs=(any_spec, vmem, vmem, vmem),
        scratch_shapes=[
            pltpu.VMEM((channels, cols), BF16),
            pltpu.VMEM((channels, cols), BF16),
            pltpu.VMEM((LATS, nlat, nlat), BF16),
            pltpu.VMEM((LATS, 2, modes, WINDOW), BF16),
            pltpu.VMEM((LATS, 2 * modes, WINDOW), BF16),
            pltpu.VMEM((LANES, cols), BF16),
            pltpu.VMEM((LANES, cols), BF16),
            pltpu.VMEM((LATS, nlat, nlat), BF16),
            pltpu.VMEM((LATS, nlat, nlat), BF16),
            pltpu.VMEM((max(1, nlat // LANES), nlat, min(LANES, nlat)), F32),
            pltpu.VMEM((LANES, hid), BF16),
            pltpu.VMEM((hid, LANES), BF16),
            pltpu.VMEM((hid, LANES), BF16),
            pltpu.VMEM((hid, LANES), F32),
            pltpu.VMEM((LATS, nlat, 2 * LANES), F32),
            pltpu.VMEM((2, nlat, LANES), F32),
            pltpu.VMEM((hid, cols), F32),
            pltpu.VMEM((LATS, 2 * modes, LANES), F32),
            pltpu.VMEM((nb * BLOCK, LANES), F32),
            pltpu.VMEM((nb * BLOCK, LANES), F32),
            pltpu.VMEM((LATS, nlat, 2 * LANES), F32),
            pltpu.VMEM((2, LANES, 2 * modes), BF16),
            pltpu.VMEM((LANES, LANES), F32),
            pltpu.VMEM((LANES, cols), BF16),
            pltpu.VMEM((hid, cols), BF16),
            pltpu.VMEM((hid, cols), BF16),
            pltpu.VMEM((LANES, cols), BF16),
            pltpu.VMEM((channels, cols), BF16),
            pltpu.VMEM((8, LANES), F32),
            pltpu.VMEM((LATS * nb, modes), BF16),
            pltpu.VMEM((8, nb, BLOCK, LANES), BF16),
            pltpu.VMEM((8, nb, BLOCK, LANES), BF16),
            pltpu.VMEM((ne, per_e, LANES), F32),
            pltpu.VMEM((ne, per_e, LANES), F32),
            pltpu.VMEM((nx, per_x, LANES), F32),
            pltpu.VMEM((nx, per_x, LANES), F32),
            pltpu.VMEM((2, per_x, LANES), F32),
            pltpu.VMEM((2, 4, per_x, LANES), F32),
            pltpu.VMEM((nx, per_x, LANES), F32),
            pltpu.VMEM((ne, per_e, LANES), F32),
            dma((7,)),
            dma((2,)),
            dma((8,)),
            dma((8,)),
            dma((4,)),
            dma((4,)),
            dma((2,)),
            dma((2,)),
        ],
        compiler_params=pltpu.CompilerParams(
            collective_id=0, has_side_effects=True, vmem_limit_bytes=60 * 1024 * 1024
        ),
    )(
        state, cotangent, legendre, jnp.asarray(trig_table(modes)), w_in, w_out, b_in,
        diffusion.reshape(1, channels), quad, quad.reshape(1, nlat), table.T, table.T,
    )
    return grad, g_in, g_out, g_b


def solution(mesh):
    nb, ne = mesh.shape["band"], mesh.shape["ens"]
    nx = 4 if nb == 64 else 2
    placed = (
        P("ens", None, "band"),
        P("ens", None, "band"),
        P(),
        P(),
        P(),
        P("band", None, None),
        P(),
        P(),
        P(),
    )
    return jax.shard_map(
        functools.partial(body, nx, nb // nx, ne),
        mesh=mesh,
        in_specs=placed,
        out_specs=(P("ens", None, "band"), P(), P(), P()),
        check_vma=False,
    )
```

```python
import functools
import math

import jax
import jax.numpy as jnp
import numpy as np
from jax import lax
from jax.experimental import pallas as pl
from jax.experimental.pallas import tpu as pltpu
from jax.sharding import PartitionSpec as P

MESH = pl.DeviceIdType.MESH
F32, BF16 = jnp.float32, jnp.bfloat16
NLON = 1440
LATS = 4
LANES = 128
STEP = 11 * LANES
WINDOW = 12 * LANES
CHUNK = 6 * LANES
BLOCK = 16


def trig_table(modes):
    phase = np.outer(np.arange(modes), np.arange(NLON)) % NLON
    angle = phase.astype(np.float64) * (2.0 * math.pi / NLON)
    both = np.stack([np.cos(angle), np.sin(angle)]) / math.sqrt(NLON)
    out = np.zeros((LATS, 2, modes, WINDOW), np.float32)
    for a in range(LATS):
        shift = a * (NLON - STEP)
        out[a, :, :, shift : shift + NLON] = both
    return out.astype(jnp.bfloat16)


def nn(a, b):
    return jnp.dot(a, b, preferred_element_type=F32)


def nt(a, b):
    return lax.dot_general(a, b, (((1,), (1,)), ((), ())), preferred_element_type=F32)


def kernel(
    nx, nz, ne,
    state_hbm, cot_hbm, leg_hbm, trig_hbm, w_in, w_out, bias, diffusion, quad, quad_row, table, table_v,
    head_hbm, lines_hbm, tail_hbm, wave_hbm, sums_hbm,
    state_raw, cot_raw, leg_raw, trig, wave, state_pad, cot_pad, leg, leg_t, leg_f, w_in_pad, w_in_t, w_out_t, b_cols,
    keep, quad_cols, hidden_grad, direct, stage_0, stage_1, partial, back_t, tail, y, hidden, pre_grad, back_grid,
    out_v, small, picks, send, recv, gt, rs1, red1, rs2, zsend, zrecv, agx, full,
    in_sem, out_sem, send_sem, recv_sem, g_send, g_recv, z_send, z_recv,
):
    nb = nx * nz
    me = lax.axis_index("band")
    ens = lax.axis_index("ens")
    my_x, my_z = me // nz, lax.rem(me, nz)
    channels = state_raw.shape[0]
    hid = w_in.shape[1]
    nlat = nb * LATS
    modes = nb * LATS
    pair = 2 * nb
    whole = channels // 16 * 16
    cols = state_raw.shape[1]
    stage = (stage_0, stage_1)

    load_state = pltpu.make_async_copy(state_hbm.at[0], state_raw, in_sem.at[0])
    load_trig = [pltpu.make_async_copy(trig_hbm.at[a], trig.at[a], in_sem.at[1 + a]) for a in range(LATS)]
    load_cot = pltpu.make_async_copy(cot_hbm.at[0], cot_raw, in_sem.at[5])
    load_leg = pltpu.make_async_copy(leg_hbm, leg_raw, in_sem.at[6])
    for load in (load_state, *load_trig[:2]):
        load.start()

    def peer_of(i):
        j, dx = i // nx, lax.rem(i, nx)
        up = (j + 1) // 2
        dz = jnp.where(lax.rem(j, 2) == 1, up, nz - up)
        return lax.rem(my_x + dx, nx) * nz + lax.rem(my_z + dz, nz)

    barrier = pltpu.get_barrier_semaphore()

    def greet_band(i, _):
        pl.semaphore_signal(barrier, inc=1, device_id=(peer_of(i), ens), device_id_type=MESH)
        return 0

    def greet_ens(i, _):
        pl.semaphore_signal(barrier, inc=1, device_id=(me, lax.rem(ens + i, ne)), device_id_type=MESH)
        return 0

    lax.fori_loop(1, nb, greet_band, 0)
    lax.fori_loop(1, ne, greet_ens, 0)

    def prepare(n, p):
        send[n] = stage[p][...].reshape(nb, BLOCK, LANES).astype(BF16)
        recv[n, pl.ds(me, 1)] = send[n, pl.ds(me, 1)]

    def start(n, first, last):
        def one(i, _):
            peer = peer_of(nb - i)
            pltpu.make_async_remote_copy(
                src_ref=send.at[n, peer],
                dst_ref=recv.at[n, me],
                send_sem=send_sem.at[n],
                recv_sem=recv_sem.at[n],
                device_id=(peer, ens),
                device_id_type=MESH,
            ).start()
            return 0

        lax.fori_loop(first, last, one, 0)

    def arrived(n, p):
        part = recv.at[n, pl.ds(0, nb - 1)]
        pltpu.make_async_copy(part, part, recv_sem.at[n]).wait()
        stage[p][...] = recv[n].astype(F32).reshape(nb * BLOCK, LANES)

    def left(n):
        part = send.at[n, pl.ds(0, nb - 1)]
        pltpu.make_async_copy(part, part, send_sem.at[n]).wait()

    def rows_of(sub, k):
        return pl.ds(sub * 8 + k, nb, stride=BLOCK)

    def pad_rows(dst, src, at):
        dst[pl.ds(0, whole), at] = src[pl.ds(0, whole), at]
        dst[pl.ds(whole, 16), at] = jnp.zeros((16, at.size), dst.dtype)
        dst[pl.ds(whole, channels - whole), at] = src[pl.ds(whole, channels - whole), at]

    def window(a):
        return pl.ds(a * STEP, WINDOW)

    small[...] = jnp.zeros_like(small)
    small[pl.ds(0, LATS), pl.ds(0, nb)] = table_v[...].astype(F32)
    turned = small[...].T
    lane = lax.broadcasted_iota(jnp.int32, (nb, modes), 1).astype(F32)
    picks[...] = jnp.concatenate(
        [(turned[:nb, s : s + 1] == lane).astype(F32) for s in range(LATS)], axis=0
    ).astype(BF16)

    load_state.wait()
    for p in range(2):
        pad_rows(state_pad, state_raw, pl.ds(p * 2 * STEP, cols - 2 * STEP if p else 2 * STEP + LANES))
        pieces = []
        for sub in range(2):
            a = 2 * p + sub
            load_trig[a].wait()
            if a == 1:
                for load in (*load_trig[2:], load_leg, load_cot):
                    load.start()
            coef = nt(trig[a].reshape(2 * modes, WINDOW), state_pad[:, window(a)])
            coef = (coef * quad[me * LATS + a]).astype(BF16)
            pieces += [coef[:modes], coef[modes:]]
        picked = nn(picks[...], jnp.concatenate(pieces, axis=1))
        for sub in range(2):
            for k in range(8):
                s, r = k // 2, k % 2
                at = (2 * sub + r) * LANES
                stage[p][rows_of(sub, k), :] = picked[s * nb : (s + 1) * nb, at : at + LANES]
        prepare(p, p)
        if p == 0:
            pl.semaphore_wait(barrier, nb - 1 + ne - 1)
        start(p, 1, nb)

    for a in range(LATS):
        for r in range(2):
            rows = nn(picks[...], trig[a, r]).astype(BF16)
            for s in range(LATS):
                wave[a, pl.ds((2 * s + r) * nb, nb), :] = rows[s * nb : (s + 1) * nb]
    load_leg.wait()
    for s in range(LATS):
        sides = []
        for side in range(leg_f.shape[0]):
            side_cols = pl.ds(side * leg_f.shape[2], leg_f.shape[2])
            leg_f[side] = leg_raw[s, :, side_cols].astype(F32)
            sides.append(
                jnp.concatenate([leg_f[side, pl.ds(a, nb, stride=LATS), :] for a in range(LATS)], axis=0)
            )
        ordered = jnp.concatenate(sides, axis=1)
        leg[s] = ordered.astype(BF16)
        leg_t[s] = ordered.T.astype(BF16)
    small[pl.ds(0, 1), :] = jnp.zeros((1, LANES), F32)
    small[pl.ds(0, 1), pl.ds(0, channels)] = diffusion[...]
    degree = lax.broadcasted_iota(jnp.int32, (nlat, LANES), 0)
    degree_f = degree.astype(F32)
    scaled = degree_f * (degree_f + 1.0) / (nlat * (nlat - 1.0))
    damp = 1.0 / (1.0 + small[pl.ds(0, 1), :] * (scaled * scaled))
    for s in range(LATS):
        kept = jnp.where(degree >= table[s, me], damp, 0.0)
        keep[s] = jnp.concatenate([kept, kept], axis=1)
    stage_quad = jnp.broadcast_to(quad_row[...], (LANES, nlat)).T
    quad_cols[0] = stage_quad
    for a in range(LATS):
        quad_cols[1, pl.ds(a * nb, nb), :] = quad_cols[0, pl.ds(a, nb, stride=LATS), :]
    b_cols[...] = jnp.broadcast_to(bias[...].reshape(1, hid), (LANES, hid)).T
    pad_rows(w_in_pad, w_out, pl.ds(0, hid))
    w_out_t[...] = w_in_pad[...].astype(F32).T.astype(BF16)
    pad_rows(w_in_pad, w_in, pl.ds(0, hid))
    w_in_t[...] = w_in_pad[...].astype(F32).T.astype(BF16)
    load_cot.wait()
    pad_rows(cot_pad, cot_raw, pl.ds(0, cols))
    for a in range(LATS):
        direct[a] = nt(wave[a], cot_pad[:, window(a)])
    wide = cols // 5

    def weigh(i, _):
        at = pl.ds(pl.multiple_of(i * wide, LANES), wide)
        hidden_grad[:, at] = nn(w_out_t[...], cot_pad[:, at])
        return 0

    lax.fori_loop(0, 5, weigh, 0)

    def legendre(n, weight, between=None, first=nb):
        def lines(p, s):
            parts = [
                jnp.concatenate([stage[p][rows_of(sub, 2 * s + r), :] for sub in range(2)], axis=0)
                for r in range(2)
            ]
            return jnp.concatenate(parts, axis=1).astype(BF16)

        arrived(n, 0)
        for s in range(LATS):
            partial[s] = nn(leg_t[s, :, pl.ds(0, pair)], lines(0, s))
        if between is not None:
            between()
        arrived(n + 1, 1)
        spectrum = []
        for s in range(LATS):
            summed = partial[s] + nn(leg_t[s, :, pl.ds(pair, pair)], lines(1, s))
            spectrum.append((summed * keep[s]).astype(BF16))
        for p in range(2):
            for s in range(LATS):
                back = nn(leg[s, pl.ds(p * pair, pair), :], spectrum[s])
                for r in range(2):
                    part = back[:, r * LANES : (r + 1) * LANES]
                    if weight:
                        part = part * quad_cols[1, pl.ds(p * pair, pair), :]
                    for sub in range(2):
                        stage[p][rows_of(sub, 2 * s + r), :] = part[sub * nb : (sub + 1) * nb]
            prepare(n + 2 + p, p)
            if p == 0 or between is None:
                start(n + 2 + p, 1, first)

    def gather(n, p):
        arrived(n, p)
        for sub in range(2):
            rows = jnp.concatenate([stage[p][rows_of(sub, k), :] for k in range(8)], axis=0)
            back_t[sub] = rows.T.astype(BF16)

    def synthesis(n, p, write):
        gather(n, p)
        held = tail[...] if p else None
        for sub in range(2):
            a = 2 * p + sub
            lines = nn(back_t[sub], wave[a])
            write(a * STEP, lines[:, :LANES] if held is None else lines[:, :LANES] + held)
            write(a * STEP + LANES, lines[:, LANES:STEP])
            held = lines[:, STEP:]
        if p == 0:
            tail[...] = held
        write((2 * p + 2) * STEP, held)

    legendre(0, False)

    def write_y(start, lines):
        row = lax.broadcasted_iota(jnp.int32, lines.shape, 0)
        lines = jnp.where(row < channels, lines, jnp.where(row == channels, 1.0, 0.0))
        y[:, pl.ds(start, lines.shape[1])] = lines.astype(BF16)

    def network(i, _):
        at = pl.ds(pl.multiple_of(i * LANES, LANES), CHUNK)
        pre = nn(w_in_t[...], y[:, at]) + jnp.concatenate([b_cols[...]] * (CHUNK // LANES), axis=1)
        sigma = 0.5 * jnp.tanh(0.5 * pre) + 0.5
        act = pre * sigma
        grad = (hidden_grad[:, at] * (sigma + act * (1.0 - sigma))).astype(BF16)
        hidden[:, at] = act.astype(BF16)
        pre_grad[:, at] = grad
        back_grid[:, at] = nn(w_in_pad[...], grad).astype(BF16)
        return 0

    per_e = 2 * hid // ne
    per_x = per_e // nx
    gt[...] = jnp.zeros_like(gt)

    def gradients(begin, width):
        def one(i, _):
            at = pl.ds(pl.multiple_of(begin + i * width, LANES), width)
            g_in = nt(pre_grad[:, at], y[:, at])
            g_out = nt(hidden[:, at], cot_pad[:, at])
            gt[...] += jnp.concatenate([g_in, g_out], axis=0).reshape(gt.shape)
            return 0

        lax.fori_loop(0, 3, one, 0)

    y[:, pl.ds(2 * STEP + LANES, LANES)] = jnp.zeros((LANES, LANES), BF16)
    tiles = cols // LANES
    per_pair, per_chunk = (tiles + 1) // 2, CHUNK // LANES
    trips = -(-per_pair // per_chunk)
    for p in range(2):
        synthesis(2 + p, p, write_y)
        begin = (tiles - trips * per_chunk) if p else 0
        lax.fori_loop(0, trips, lambda i, c, begin=begin: network(begin + i * per_chunk, c), 0)
        for sub in range(2):
            a = 2 * p + sub
            coef = direct[a] + nt(wave[a], back_grid[:, window(a)])
            for k in range(8):
                stage[p][rows_of(sub, k), :] = coef[k * nb : (k + 1) * nb]
        prepare(4 + p, p)
        if p == 0:
            start(4, 1, nb)
            gradients(0, (tiles - trips * per_chunk) * LANES // 3)
        else:
            gradients(begin * LANES, trips * CHUNK // 3)

    def to_ens(src, dst, n):
        def one(i, _):
            other = lax.rem(ens + i, ne)
            pltpu.make_async_remote_copy(
                src_ref=src(other), dst_ref=dst, send_sem=g_send.at[n], recv_sem=g_recv.at[n],
                device_id=(me, other), device_id_type=MESH,
            ).start()
            return 0

        lax.fori_loop(1, ne, one, 0)

    def to_x(src, dst, n):
        def one(i, _):
            other = lax.rem(my_x + i, nx)
            pltpu.make_async_remote_copy(
                src_ref=src(other), dst_ref=dst, send_sem=g_send.at[n], recv_sem=g_recv.at[n],
                device_id=(other * nz + my_z, ens), device_id_type=MESH,
            ).start()
            return 0

        lax.fori_loop(1, nx, one, 0)

    z_sizes = (4, nz // 4)

    def to_z(step, value):
        stride = 4**step
        digit = lax.rem(my_z // stride, z_sizes[step])
        zrecv[step, pl.ds(digit, 1)] = value[None]
        zsend[step] = value

        def one(i, _):
            other = my_z + (lax.rem(digit + i, z_sizes[step]) - digit) * stride
            pltpu.make_async_remote_copy(
                src_ref=zsend.at[step], dst_ref=zrecv.at[step, digit], send_sem=z_send.at[step],
                recv_sem=z_recv.at[step], device_id=(my_x * nz + other, ens), device_id_type=MESH,
            ).start()
            return 0

        lax.fori_loop(1, z_sizes[step], one, 0)

    def from_z(step):
        if z_sizes[step] > 1:
            took(zrecv.at[step], z_sizes[step] - 1, z_recv.at[step])
        return jnp.sum(zrecv[step, pl.ds(0, z_sizes[step])], axis=0)

    def took(ref, count, sem):
        part = ref.at[pl.ds(0, count)]
        pltpu.make_async_copy(part, part, sem).wait()

    rs1[pl.ds(ens, 1)] = gt[pl.ds(ens, 1)]
    to_ens(lambda other: gt.at[other], rs1.at[ens], 0)
    start(5, 1, 5 * nb // 8)
    took(rs1, ne - 1, g_recv.at[0])
    red1[...] = jnp.sum(rs1[...], axis=0).reshape(nx, per_x, LANES)
    rs2[pl.ds(my_x, 1)] = red1[pl.ds(my_x, 1)]
    to_x(lambda other: red1.at[other], rs2.at[my_x], 1)
    start(5, 5 * nb // 8, nb)

    def first_z():
        took(rs2, nx - 1, g_recv.at[1])
        to_z(0, jnp.sum(rs2[...], axis=0))

    legendre(4, True, first_z, 3 * nb // 8)
    to_z(1, from_z(0))
    start(6, 3 * nb // 8, 7 * nb // 8)
    agx[pl.ds(my_x, 1)] = from_z(1)[None]
    to_x(lambda other: agx.at[my_x], agx.at[my_x], 2)
    start(6, 7 * nb // 8, nb)
    start(7, 1, nb // 2)
    took(agx, nx - 1, g_recv.at[2])
    full[pl.ds(ens, 1)] = agx[...].reshape(1, per_e, LANES)
    to_ens(lambda other: full.at[ens], full.at[ens], 3)
    start(7, nb // 2, nb)

    def write_out(start, lines):
        out_v[:, pl.ds(start, lines.shape[1])] = lines[:channels].astype(BF16)

    keep_wave = pltpu.make_async_copy(wave.at[pl.ds(2, 2)], wave_hbm, out_sem.at[0])
    keep_wave.start()
    synthesis(6, 0, write_out)
    head = pltpu.make_async_copy(out_v.at[:, pl.ds(0, 2 * STEP)], head_hbm, out_sem.at[1])
    head.start()
    keep_tail = pltpu.make_async_copy(tail, tail_hbm, out_sem.at[2])
    keep_tail.start()
    took(full, ne - 1, g_recv.at[3])
    keep_sums = pltpu.make_async_copy(full, sums_hbm, out_sem.at[3])
    keep_sums.start()
    for n in range(6):
        left(n)
    took(gt, ne - 1, g_send.at[0])
    took(red1, nx - 1, g_send.at[1])
    took(agx, nx - 1, g_send.at[2])
    took(full, ne - 1, g_send.at[3])
    for step in range(2):
        if z_sizes[step] > 1:
            took(zrecv.at[step], z_sizes[step] - 1, z_send.at[step])
    left(6)
    left(7)
    keep_wave.wait()
    head.wait()
    keep_tail.wait()
    keep_sums.wait()
    gather(7, 1)
    keep_lines = pltpu.make_async_copy(back_t, lines_hbm, out_sem.at[4])
    keep_lines.start()
    keep_lines.wait()


def last_kernel(
    scale, head_hbm, lines_hbm, tail_hbm, wave_hbm, sums_hbm, grad_hbm, w_in_grad, w_out_grad, b_grad,
    lines_v, tail, wave, sums, out_v, sem,
):
    channels = out_v.shape[0]
    hid = w_in_grad.shape[1]
    front, rear = pl.ds(0, 2 * STEP), pl.ds(2 * STEP, out_v.shape[1] - 2 * STEP)
    head = pltpu.make_async_copy(head_hbm, out_v.at[:, front], sem.at[0])
    store_0 = pltpu.make_async_copy(out_v.at[:, front], grad_hbm.at[0, :, front], sem.at[7])
    store_1 = pltpu.make_async_copy(out_v.at[:, rear], grad_hbm.at[0, :, rear], sem.at[6])
    loads = [
        pltpu.make_async_copy(lines_hbm, lines_v, sem.at[1]),
        pltpu.make_async_copy(wave_hbm.at[0], wave.at[0], sem.at[2]),
        pltpu.make_async_copy(tail_hbm, tail, sem.at[3]),
        pltpu.make_async_copy(wave_hbm.at[1], wave.at[1], sem.at[4]),
        pltpu.make_async_copy(sums_hbm, sums, sem.at[5]),
    ]
    for load in loads:
        load.start()
    head.start()
    loads[0].wait()
    loads[1].wait()
    loads[2].wait()
    held = tail[...]
    for sub in range(2):
        if sub == 1:
            head.wait()
            store_0.start()
            loads[3].wait()
        lines = nn(lines_v[sub], wave[sub])
        first = (lines[:, :LANES] + held)[:channels].astype(BF16)
        out_v[:, pl.ds((2 + sub) * STEP, LANES)] = first
        out_v[:, pl.ds((2 + sub) * STEP + LANES, STEP - LANES)] = lines[:channels, LANES:STEP].astype(BF16)
        held = lines[:, STEP:]
    out_v[:, pl.ds(4 * STEP, LANES)] = held[:channels].astype(BF16)
    store_1.start()
    loads[4].wait()
    scaled = (sums[...] * scale).reshape(2 * hid, LANES)
    g_in, g_out = scaled[:hid].T, scaled[hid:].T
    w_in_grad[...] = g_in[:channels]
    w_out_grad[...] = g_out[:channels]
    b_grad[...] = g_in[channels]
    store_0.wait()
    store_1.wait()


def body(nx, nz, ne, state, cotangent, w_in, b_in, w_out, legendre, diffusion, quad, table):
    nb = nx * nz
    channels, cols = state.shape[1:]
    hid = w_in.shape[1]
    nlat = legendre.shape[1]
    modes = nb * LATS
    per_e = 2 * hid // ne
    per_x = per_e // nx
    scale = 1.0 / math.sqrt(ne * nlat * NLON)
    any_spec = pl.BlockSpec(memory_space=pl.ANY)
    vmem = pl.BlockSpec(memory_space=pltpu.VMEM)
    smem = pl.BlockSpec(memory_space=pltpu.SMEM)
    dma = pltpu.SemaphoreType.DMA
    parts = pl.pallas_call(
        functools.partial(kernel, nx, nz, ne),
        out_shape=(
            jax.ShapeDtypeStruct((channels, 2 * STEP), BF16),
            jax.ShapeDtypeStruct((2, LANES, 2 * modes), BF16),
            jax.ShapeDtypeStruct((LANES, LANES), F32),
            jax.ShapeDtypeStruct((2, 2 * modes, WINDOW), BF16),
            jax.ShapeDtypeStruct((ne, per_e, LANES), F32),
        ),
        in_specs=[any_spec] * 4 + [vmem] * 4 + [smem, vmem, smem, vmem],
        out_specs=(any_spec,) * 5,
        scratch_shapes=[
            pltpu.VMEM((channels, cols), BF16),
            pltpu.VMEM((channels, cols), BF16),
            pltpu.VMEM((LATS, nlat, nlat), BF16),
            pltpu.VMEM((LATS, 2, modes, WINDOW), BF16),
            pltpu.VMEM((LATS, 2 * modes, WINDOW), BF16),
            pltpu.VMEM((LANES, cols), BF16),
            pltpu.VMEM((LANES, cols), BF16),
            pltpu.VMEM((LATS, nlat, nlat), BF16),
            pltpu.VMEM((LATS, nlat, nlat), BF16),
            pltpu.VMEM((max(1, nlat // LANES), nlat, min(LANES, nlat)), F32),
            pltpu.VMEM((LANES, hid), BF16),
            pltpu.VMEM((hid, LANES), BF16),
            pltpu.VMEM((hid, LANES), BF16),
            pltpu.VMEM((hid, LANES), F32),
            pltpu.VMEM((LATS, nlat, 2 * LANES), F32),
            pltpu.VMEM((2, nlat, LANES), F32),
            pltpu.VMEM((hid, cols), F32),
            pltpu.VMEM((LATS, 2 * modes, LANES), F32),
            pltpu.VMEM((nb * BLOCK, LANES), F32),
            pltpu.VMEM((nb * BLOCK, LANES), F32),
            pltpu.VMEM((LATS, nlat, 2 * LANES), F32),
            pltpu.VMEM((2, LANES, 2 * modes), BF16),
            pltpu.VMEM((LANES, LANES), F32),
            pltpu.VMEM((LANES, cols), BF16),
            pltpu.VMEM((hid, cols), BF16),
            pltpu.VMEM((hid, cols), BF16),
            pltpu.VMEM((LANES, cols), BF16),
            pltpu.VMEM((channels, cols), BF16),
            pltpu.VMEM((8, LANES), F32),
            pltpu.VMEM((LATS * nb, modes), BF16),
            pltpu.VMEM((8, nb, BLOCK, LANES), BF16),
            pltpu.VMEM((8, nb, BLOCK, LANES), BF16),
            pltpu.VMEM((ne, per_e, LANES), F32),
            pltpu.VMEM((ne, per_e, LANES), F32),
            pltpu.VMEM((nx, per_x, LANES), F32),
            pltpu.VMEM((nx, per_x, LANES), F32),
            pltpu.VMEM((2, per_x, LANES), F32),
            pltpu.VMEM((2, 4, per_x, LANES), F32),
            pltpu.VMEM((nx, per_x, LANES), F32),
            pltpu.VMEM((ne, per_e, LANES), F32),
            dma((7,)),
            dma((5,)),
            dma((8,)),
            dma((8,)),
            dma((4,)),
            dma((4,)),
            dma((2,)),
            dma((2,)),
        ],
        compiler_params=pltpu.CompilerParams(
            collective_id=0, has_side_effects=True, vmem_limit_bytes=60 * 1024 * 1024
        ),
    )(
        state, cotangent, legendre, jnp.asarray(trig_table(modes)), w_in, w_out, b_in,
        diffusion.reshape(1, channels), quad, quad.reshape(1, nlat), table.T, table.T,
    )
    return pl.pallas_call(
        functools.partial(last_kernel, scale),
        out_shape=(
            jax.ShapeDtypeStruct((1, channels, cols), BF16),
            jax.ShapeDtypeStruct((channels, hid), F32),
            jax.ShapeDtypeStruct((channels, hid), F32),
            jax.ShapeDtypeStruct((hid,), F32),
        ),
        in_specs=[any_spec] * 5,
        out_specs=(any_spec, vmem, vmem, vmem),
        scratch_shapes=[
            pltpu.VMEM((2, LANES, 2 * modes), BF16),
            pltpu.VMEM((LANES, LANES), F32),
            pltpu.VMEM((2, 2 * modes, WINDOW), BF16),
            pltpu.VMEM((ne, per_e, LANES), F32),
            pltpu.VMEM((channels, cols), BF16),
            dma((8,)),
        ],
        compiler_params=pltpu.CompilerParams(vmem_limit_bytes=60 * 1024 * 1024),
    )(*parts)


def solution(mesh):
    nb, ne = mesh.shape["band"], mesh.shape["ens"]
    nx = 4 if nb == 64 else 2
    placed = (
        P("ens", None, "band"),
        P("ens", None, "band"),
        P(),
        P(),
        P(),
        P("band", None, None),
        P(),
        P(),
        P(),
    )
    return jax.shard_map(
        functools.partial(body, nx, nb // nx, ne),
        mesh=mesh,
        in_specs=placed,
        out_specs=(P("ens", None, "band"), P(), P(), P()),
        check_vma=False,
    )
```
